32 devices in a mesh: row: 8 (over y, x, core), col: 4 (over z).
Axes of the slice: x: 2, y: 2, z: 4, core: 2. Of those that a mesh axis runs over, the one named last changes fastest.
Arguments:
- orbitals: bfloat16 [6144, 2, 2048], P(('row', 'col')), may hold values from -6 to 6
- applied_orbitals: bfloat16 [6144, 2, 2048], P(('row', 'col')), may hold values from -6 to 6
- ritz_matrix: bfloat16 [2, 2048, 2048], P(None, 'row', 'col'), may hold values from -0.09375 to 0.09375
Outputs:
- rotated_orbitals: bfloat16 [6144, 2, 2048], P(('row', 'col'))
- rotated_applied: bfloat16 [6144, 2, 2048], P(('row', 'col'))
The draws below stay inside these ranges and needn't reach their ends.
All inputs are finite; a program needn't handle non-finite values.
Results may differ from the reference program's by a relative error of at most 0.001.
Values may be sent and summed in bfloat16 or wider, within the bound.
No kernel may reach another device: no remote copies, remote signals or barrier semaphores. Data moves between devices by JAX's collectives and lax.ppermute only.
A program may use at most 128 MiB of HBM per device.

```python
import jax
import jax.numpy as jnp

NB = 2048
NG = 6144


def level_of(own_key, dims, cuts, low, top_value):
    level, own = 1.0, jax.random.fold_in(own_key, 6)
    for dim, parts in cuts:
        draws = jnp.exp(jax.random.uniform(jax.random.fold_in(own, dim), (parts,), jnp.float32, low / len(cuts), top_value / len(cuts)))
        level = level * jnp.repeat(draws, dims[dim] // parts).reshape([-1 if axis == dim else 1 for axis in range(len(dims))])
    return level


def bell_draw(rng, extent, spread, most, cuts=(), held_as=jnp.bfloat16):
    result = jax.random.normal(rng, extent, jnp.float32) * spread
    if len(cuts) > 0:
        result = level_of(rng, extent, cuts, -0.22, 0.18) * result
    return jnp.clip(result, min=-most, max=most).astype(held_as)


def setup_inputs(seed: int = 0) -> dict:
    arg_keys = jax.random.split(jax.random.key(seed), 4)
    orbitals = bell_draw(arg_keys[0], (NG, 2, NB), 1.0, 6.0, ((0, 32),))
    applied_orbitals = bell_draw(arg_keys[1], (NG, 2, NB), 1.0, 6.0, ((0, 32),))
    ritz_matrix = bell_draw(arg_keys[2], (2, NB, NB), (2 * NB) ** -0.5, 0.09375, ((1, 8), (2, 4)))
    return dict(orbitals=orbitals, applied_orbitals=applied_orbitals, ritz_matrix=ritz_matrix)


def rotate(wavefunction, ritz_matrix):
    row_count = wavefunction.shape[0]
    flattened = wavefunction.reshape(row_count, 2 * NB)
    real_part = ritz_matrix[0]
    imag_part = ritz_matrix[1]
    upper_half = jnp.concatenate([real_part, imag_part], 1)
    lower_half = jnp.concatenate([-imag_part, real_part], 1)
    real_block = jnp.concatenate([upper_half, lower_half], 0)
    product = jnp.dot(flattened, real_block, preferred_element_type=jnp.float32)
    return product.reshape(row_count, 2, NB).astype(jnp.bfloat16)


def reference(orbitals, applied_orbitals, ritz_matrix):
    return rotate(orbitals, ritz_matrix), rotate(applied_orbitals, ritz_matrix)
```

```python
import functools

import jax
import jax.numpy as jnp
from jax import lax
from jax.experimental import pallas as pl
from jax.experimental.pallas import tpu as pltpu
from jax.sharding import PartitionSpec as P

AXES = ("row", "col")


def chip_at(place, chips):
    place = place % chips
    return 2 * place if 2 * place < chips else 2 * (chips - 1 - place) + 1


class Moves:
    def __init__(self, rows, cols):
        self.chips, self.cols = rows // 2, cols

    def every(self):
        for place in range(self.chips):
            for core in range(2):
                for layer in range(self.cols):
                    yield place, core, layer

    def device(self, place, core, layer):
        return (chip_at(place, self.chips) * 2 + core) * self.cols + layer % self.cols

    def ring(self, value, step):
        pairs = [(self.device(p, k, z), self.device(p + (step if k == 0 else -step), k, z)) for p, k, z in self.every()]
        return lax.ppermute(value, AXES, pairs)

    def up(self, value):
        pairs = [(self.device(p, k, z), self.device(p, k, z + 1)) for p, k, z in self.every()]
        return lax.ppermute(value, AXES, pairs)

    def other(self, value):
        pairs = [(self.device(p, k, z), self.device(p, 1 - k, z)) for p, k, z in self.every()]
        return lax.ppermute(value, AXES, pairs)


def after(value, *earlier):
    return lax.optimization_barrier((value,) + earlier)[0]


def stage_kernel(hops, rows, cols, stage, fresh, lhs, *refs):
    count = 2 * len(hops)
    blocks = refs[:count]
    first_out, second_out, first_tile, second_tile, sems = refs[count if fresh else count + 2 :]
    chips = rows // 2
    g = first_tile.shape[0]
    depth, width = blocks[0].shape[1:]
    row, layer = lax.axis_index("row"), lax.axis_index("col")
    chip, core = row // 2, row % 2
    place = jnp.where(chip % 2 == 0, chip // 2, chips - 1 - chip // 2)
    total = jnp.zeros((4 * g, width), jnp.float32)
    for i, block in enumerate(blocks):
        hop = hops[i % len(hops)]
        owner_core = core if i < len(hops) else 1 - core
        at = (place + chips + jnp.where(owner_core == 0, -hop, hop)) % chips
        owner = jnp.where(2 * at < chips, 2 * at, 2 * (chips - 1 - at) + 1) * 2 + owner_core
        k = pl.ds(pl.multiple_of(owner * depth, depth), depth)
        total += jnp.dot(lhs[2 * g :, k], block[0], preferred_element_type=jnp.float32)
        total += jnp.dot(lhs[: 4 * g, k], block[1], preferred_element_type=jnp.float32)
    rounded = total.astype(jnp.bfloat16)
    first_tile[:, 0, :] = rounded[:g]
    first_tile[:, 1, :] = rounded[2 * g : 3 * g]
    second_tile[:, 0, :] = rounded[g : 2 * g]
    second_tile[:, 1, :] = rounded[3 * g :]
    columns = pl.ds(pl.multiple_of(((layer + cols - stage) % cols) * width, width), width)
    copies = [
        pltpu.make_async_copy(first_tile, first_out.at[:, :, columns], sems.at[0]),
        pltpu.make_async_copy(second_tile, second_out.at[:, :, columns], sems.at[1]),
    ]
    for copy in copies:
        copy.start()
    for copy in copies:
        copy.wait()


def run_stage(hops, rows, cols, stage, outs, lhs, blocks, like):
    fresh = outs is None
    g, _, bands = like.shape
    depth, width = blocks[0].shape[1:]
    vmem, hbm = pl.BlockSpec(memory_space=pltpu.VMEM), pl.BlockSpec(memory_space=pl.ANY)
    count = len(blocks)
    flops = 2 * 4 * g * 2 * depth * width * count
    return pl.pallas_call(
        functools.partial(stage_kernel, hops, rows, cols, stage, fresh),
        out_shape=(jax.ShapeDtypeStruct(like.shape, like.dtype),) * 2,
        in_specs=[vmem] * (1 + count) + ([] if fresh else [hbm] * 2),
        out_specs=(hbm, hbm),
        scratch_shapes=[pltpu.VMEM((g, 2, width), like.dtype)] * 2 + [pltpu.SemaphoreType.DMA((2,))],
        input_output_aliases={} if fresh else {1 + count: 0, 2 + count: 1},
        compiler_params=pltpu.CompilerParams(vmem_limit_bytes=24 * 2**20),
        cost_estimate=pl.CostEstimate(flops=flops, bytes_accessed=8 * 2**20, transcendentals=0),
    )(lhs, *blocks, *(() if fresh else outs))


def shards(rows, cols, orbitals, applied, ritz):
    moves = Moves(rows, cols)
    chips = rows // 2
    ahead, back = chips // 2, (chips - 1) // 2
    hops = [0, *range(1, ahead + 1), *(-h for h in range(1, back + 1))]

    real = jnp.concatenate([orbitals[:, 0], applied[:, 0]], 0)
    imag = jnp.concatenate([orbitals[:, 1], applied[:, 1]], 0)
    lhs = jnp.concatenate([-imag, real, imag], 0)

    def chain(first, count, step, *earlier):
        out = []
        for _ in range(count):
            first = moves.ring(after(first, *earlier) if earlier else first, step)
            out.append(first)
        return out

    own_ahead, own_back = chain(ritz, ahead, 1), chain(ritz, back, -1)
    layers = [ritz]
    for s in range(1, cols):
        layers.append(moves.up(layers[-1] if s == 1 else after(layers[-1], own_ahead[0], *own_back[:1])))
    stages = [[ritz, *own_ahead, *own_back]]
    if cols > 1:
        near_back = chain(after(layers[1], own_ahead[0], *own_back[:1]), back, -1)
        gate = (own_ahead[-1], *near_back[-1:])
        rings = {}
        for s in range(2, cols):
            source = after(layers[s], *gate)
            a, b = chain(source, ahead, 1), chain(source, back, -1)
            rings[s] = [layers[s], *a, *b]
            gate = (a[0], *b[-1:])
        near_ahead = []
        gate = (layers[-1],)
        for value in own_ahead:
            near_ahead.append(moves.up(after(value, *gate)))
            gate = (near_ahead[-1],)
        stages.append([layers[1], *near_ahead, *near_back])
        stages.extend(rings[s] for s in range(2, cols))
    outs = None
    for s in [0, *range(2, cols), 1][: cols]:
        blocks = stages[s]
        outs = run_stage(hops, rows, cols, s, outs, lhs, [*blocks, *map(moves.other, blocks)], orbitals)
    return outs


def solution(mesh):
    rows, cols = mesh.shape["row"], mesh.shape["col"]
    whole = P(AXES, None, None)
    return jax.shard_map(
        functools.partial(shards, rows, cols),
        mesh=mesh,
        in_specs=(whole, whole, P(None, "row", "col")),
        out_specs=(whole, whole),
        check_vma=False,
    )
```

```python
import functools

import jax
import jax.numpy as jnp
from jax import lax
from jax.experimental import pallas as pl
from jax.experimental.pallas import tpu as pltpu
from jax.sharding import PartitionSpec as P

AXES = ("row", "col")


def chip_at(place, chips):
    place = place % chips
    return 2 * place if 2 * place < chips else 2 * (chips - 1 - place) + 1


class Moves:
    def __init__(self, rows, cols):
        self.chips, self.cols = rows // 2, cols

    def every(self):
        for place in range(self.chips):
            for core in range(2):
                for layer in range(self.cols):
                    yield place, core, layer

    def device(self, place, core, layer):
        return (chip_at(place, self.chips) * 2 + core) * self.cols + layer % self.cols

    def ring(self, value, step):
        pairs = [(self.device(p, k, z), self.device(p + (step if k == 0 else -step), k, z)) for p, k, z in self.every()]
        return lax.ppermute(value, AXES, pairs)

    def along(self, value, step):
        pairs = [(self.device(p, k, z), self.device(p, k, z + step)) for p, k, z in self.every()]
        return lax.ppermute(value, AXES, pairs)

    def other(self, value):
        pairs = [(self.device(p, k, z), self.device(p, 1 - k, z)) for p, k, z in self.every()]
        return lax.ppermute(value, AXES, pairs)


def after(value, *earlier):
    return lax.optimization_barrier((value,) + earlier)[0]


class Part:
    def __init__(self, stage, terms, begun=None, finish=True):
        self.stage, self.terms, self.begun, self.finish = stage, terms, begun, finish


def parts_kernel(plan, rows, cols, n_arrays, n_outs, fresh, first, second, *refs):
    refs = list(refs)
    arrays = [refs.pop(0) for _ in range(n_arrays)]
    begun = [refs.pop(0) if has else None for _, _, has, _ in plan]
    if n_outs and not fresh:
        del refs[:2]
    outs = [refs.pop(0) for _ in range(n_outs)]
    sums = [None if finish else refs.pop(0) for _, _, _, finish in plan]
    chips = rows // 2
    depth, width = arrays[0].shape[1:]
    g, bands = first.shape[0], first.shape[1] // 2
    row, layer = lax.axis_index("row"), lax.axis_index("col")
    chip, core = row // 2, row % 2
    place = jnp.where(chip % 2 == 0, chip // 2, chips - 1 - chip // 2)
    copies = []
    for i, (stage, terms, _, finish) in enumerate(plan):
        total = jnp.zeros((4 * g, width), jnp.float32) if begun[i] is None else begun[i][...]
        for hop, mine, array, number in terms:
            owner_core = core if mine else 1 - core
            at = (place + chips + jnp.where(owner_core == 0, -hop, hop)) % chips
            owner = jnp.where(2 * at < chips, 2 * at, 2 * (chips - 1 - at) + 1) * 2 + owner_core
            real = pl.ds(pl.multiple_of(owner * depth, depth), depth)
            imag = pl.ds(pl.multiple_of(bands + owner * depth, depth), depth)
            left = [jnp.concatenate([x[:, real], -x[:, imag]], 1) for x in (first, second)]
            left += [jnp.concatenate([x[:, imag], x[:, real]], 1) for x in (first, second)]
            right = arrays[array][2 * number : 2 * number + 2].reshape(2 * depth, width)
            total += jnp.dot(jnp.concatenate(left, 0), right, preferred_element_type=jnp.float32)
        if not finish:
            sums[i][...] = total
            continue
        rounded = total.astype(outs[0].dtype)
        columns = pl.ds(pl.multiple_of(((layer + cols - stage) % cols) * width, width), width)
        for half in range(2):
            tile, sem = refs.pop(0), refs.pop(0)
            tile[:, 0, :] = rounded[half * g : (half + 1) * g]
            tile[:, 1, :] = rounded[(2 + half) * g : (3 + half) * g]
            copy = pltpu.make_async_copy(tile, outs[half].at[:, :, columns], sem)
            copy.start()
            copies.append(copy)
    for copy in copies:
        copy.wait()


def run_parts(parts, rows, cols, lefts, like, outs=None):
    g = like.shape[0]
    fresh = outs is None
    finishing = sum(p.finish for p in parts)
    vmem, hbm = pl.BlockSpec(memory_space=pltpu.VMEM), pl.BlockSpec(memory_space=pl.ANY)
    arrays = list({id(t[2]): t[2] for p in parts for t in p.terms}.values())
    index = {id(a): i for i, a in enumerate(arrays)}
    depth, width = arrays[0].shape[1:]
    operands = [*lefts, *arrays, *(p.begun for p in parts if p.begun is not None)]
    in_specs = [vmem] * len(operands)
    out_shape, out_specs, scratch, aliases = [], [], [], {}
    if finishing:
        if not fresh:
            aliases = {len(operands): 0, len(operands) + 1: 1}
            operands, in_specs = [*operands, *outs], [*in_specs, hbm, hbm]
        out_shape, out_specs = [jax.ShapeDtypeStruct(like.shape, like.dtype)] * 2, [hbm, hbm]
        scratch = [pltpu.VMEM((g, 2, width), like.dtype), pltpu.SemaphoreType.DMA] * 2 * finishing
    sums = len(parts) - finishing
    out_shape += [jax.ShapeDtypeStruct((4 * g, width), jnp.float32)] * sums
    out_specs += [vmem] * sums
    count = sum(len(p.terms) for p in parts)
    plan = [(p.stage, [(h, m, index[id(a)], n) for h, m, a, n in p.terms], p.begun is not None, p.finish) for p in parts]
    result = pl.pallas_call(
        functools.partial(parts_kernel, plan, rows, cols, len(arrays), 2 if finishing else 0, fresh),
        out_shape=out_shape,
        in_specs=in_specs,
        out_specs=out_specs,
        scratch_shapes=scratch,
        input_output_aliases=aliases,
        compiler_params=pltpu.CompilerParams(vmem_limit_bytes=28 * 2**20),
        cost_estimate=pl.CostEstimate(flops=2 * 8 * g * depth * width * count, bytes_accessed=2**20 * count, transcendentals=0),
    )(*operands)
    return (tuple(result[:2]), result[2:]) if finishing else (outs, result)


def shards(rows, cols, orbitals, applied, ritz):
    moves = Moves(rows, cols)
    chips = rows // 2
    ahead, back = chips // 2, (chips - 1) // 2
    hops = [*range(ahead + 1), *(-h for h in range(1, back + 1))]
    lefts = [x.reshape(x.shape[0], -1) for x in (orbitals, applied)]
    run = functools.partial(run_parts, rows=rows, cols=cols, lefts=lefts, like=orbitals)

    final = cols + chips - 3
    distances = [*range(cols - 1), -1]
    mine, theirs = {(0, 0): (ritz, 0)}, {}

    def bundle(keys, gate):
        values = [lax.slice_in_dim(a, 2 * n, 2 * n + 2) if a.shape[0] > 2 else a for a, n in (mine[key] for key in keys)]
        if gate:
            values = [after(v, *gate) for v in values]
        return jnp.concatenate(values, 0) if len(values) > 1 else values[0]

    def move(how, into, sources, keys, gate, name):
        if not keys:
            return ()
        with jax.named_scope(name):
            value = how(bundle(sources, gate))
        into.update({key: (value, number) for number, key in enumerate(keys)})
        return (value,)

    def part(layer, hops, begun=None, finish=True):
        return Part(layer, [(h, whose is mine, *whose[layer, h]) for whose in (mine, theirs) for h in hops], begun, finish)

    def complete(layer):
        return [*range(chips - 1), -1] if layer in (0, -1) else [*range(chips)]

    state = {"outs": None}
    sums, used = {}, {d: [] for d in distances}

    def products(keys):
        parts = []
        for d in distances:
            hops = [h for h in complete(d) if (d, h) in keys and h not in used[d]]
            if hops:
                used[d] += hops
                parts.append(part(d, hops, sums.pop(d, None), len(used[d]) == len(complete(d))))
        parts.sort(key=lambda p: p.finish)
        state["outs"], kept = run(parts, outs=state["outs"])
        unfinished = [p for p in parts if not p.finish]
        sums.update({p.stage: s for p, s in zip(unfinished, kept, strict=True)})
        return kept[0] if unfinished else state["outs"][0]

    def tiny(value, number):
        at = 16 * (number % (ritz.shape[1] // 16))
        with jax.named_scope("token"):
            return moves.other(after(lax.slice(ritz, (0, at, 0), (1, at + 16, 128)), value))

    along_gate = gate = ()
    fresh = [(0, 0)]
    for r in range(1, final + 1):
        if r < cols - 1:
            layer, hop, step = r, 0, 1
        else:
            layer, hop, step = -1, r - (cols - 1), -1
        source = (layer - step, hop)
        z = move(lambda v: moves.along(v, step), mine, [source], [(layer, hop)], along_gate, f"along{layer}_{hop}")
        ring = [(d, r - d) for d in range(cols - 1) if 1 <= r - d <= (chips - 2 if d == 0 else chips - 1)]
        p = move(lambda v: moves.ring(v, 1), mine, [(d, h - 1) for d, h in ring], ring, gate, f"ring{r}")
        back = {1: [(0, -1)], final: [(-1, -1)]}.get(r, [])
        m = move(lambda v: moves.ring(v, -1), mine, [(d, 0) for d, _ in back], back, gate, f"back{r}")
        e = move(moves.other, theirs, fresh, fresh, gate, f"core{r}")
        fresh_before, fresh = fresh, [*ring, (layer, hop), *back]
        token = ()
        held = set(theirs) - set(fresh_before)
        if r >= chips:
            ran = products(held)
            if r == final:
                ran = products(set(theirs))
            token = (tiny(ran, r),)
        along_gate = (*p, *m, *e, *token, *(lefts if r == 1 else ()))
        gate = (*along_gate, *z)
    move(moves.other, theirs, fresh, fresh, token, "core_last")
    products(set(theirs))
    return state["outs"]


def solution(mesh):
    rows, cols = mesh.shape["row"], mesh.shape["col"]
    whole = P(AXES, None, None)
    return jax.shard_map(
        functools.partial(shards, rows, cols),
        mesh=mesh,
        in_specs=(whole, whole, P(None, "row", "col")),
        out_specs=(whole, whole),
        check_vma=False,
    )
```

```python
import functools

import jax
import jax.numpy as jnp
from jax import lax
from jax.experimental import pallas as pl
from jax.experimental.pallas import tpu as pltpu
from jax.sharding import PartitionSpec as P

AXES = ("row", "col")


def chip_at(place, chips):
    place = place % chips
    return 2 * place if 2 * place < chips else 2 * (chips - 1 - place) + 1


class Moves:
    def __init__(self, rows, cols):
        self.chips, self.cols = rows // 2, cols

    def every(self):
        for place in range(self.chips):
            for core in range(2):
                for layer in range(self.cols):
                    yield place, core, layer

    def device(self, place, core, layer):
        return (chip_at(place, self.chips) * 2 + core) * self.cols + layer % self.cols

    def ring(self, value, step):
        pairs = [(self.device(p, k, z), self.device(p + (step if k == 0 else -step), k, z)) for p, k, z in self.every()]
        return lax.ppermute(value, AXES, pairs)

    def along(self, value, step):
        pairs = [(self.device(p, k, z), self.device(p, k, z + step)) for p, k, z in self.every()]
        return lax.ppermute(value, AXES, pairs)

    def other(self, value):
        pairs = [(self.device(p, k, z), self.device(p, 1 - k, z)) for p, k, z in self.every()]
        return lax.ppermute(value, AXES, pairs)


def after(value, *earlier):
    return lax.optimization_barrier((value,) + earlier)[0]


class Part:
    def __init__(self, stage, terms, begun=None, finish=True):
        self.stage, self.terms, self.begun, self.finish = stage, terms, begun, finish


def parts_kernel(plan, rows, cols, n_arrays, n_outs, fresh, first, second, *refs):
    refs = list(refs)
    arrays = [refs.pop(0) for _ in range(n_arrays)]
    begun = [refs.pop(0) if has else None for _, _, has, _ in plan]
    if n_outs and not fresh:
        del refs[:2]
    outs = [refs.pop(0) for _ in range(n_outs)]
    sums = [None if finish else refs.pop(0) for _, _, _, finish in plan]
    chips = rows // 2
    depth, width = arrays[0].shape[1:]
    g, bands = first.shape[0], first.shape[1] // 2
    row, layer = lax.axis_index("row"), lax.axis_index("col")
    chip, core = row // 2, row % 2
    place = jnp.where(chip % 2 == 0, chip // 2, chips - 1 - chip // 2)
    copies = []
    for i, (stage, terms, _, finish) in enumerate(plan):
        total = jnp.zeros((4 * g, width), jnp.float32) if begun[i] is None else begun[i][...]
        for hop, mine, array, number in terms:
            owner_core = core if mine else 1 - core
            at = (place + chips + jnp.where(owner_core == 0, -hop, hop)) % chips
            owner = jnp.where(2 * at < chips, 2 * at, 2 * (chips - 1 - at) + 1) * 2 + owner_core
            real = pl.ds(pl.multiple_of(owner * depth, depth), depth)
            imag = pl.ds(pl.multiple_of(bands + owner * depth, depth), depth)
            left = [jnp.concatenate([x[:, real], -x[:, imag]], 1) for x in (first, second)]
            left += [jnp.concatenate([x[:, imag], x[:, real]], 1) for x in (first, second)]
            right = arrays[array][2 * number : 2 * number + 2].reshape(2 * depth, width)
            total += jnp.dot(jnp.concatenate(left, 0), right, preferred_element_type=jnp.float32)
        if not finish:
            sums[i][...] = total
            continue
        rounded = total.astype(outs[0].dtype)
        columns = pl.ds(pl.multiple_of(((layer + cols - stage) % cols) * width, width), width)
        for half in range(2):
            tile, sem = refs.pop(0), refs.pop(0)
            tile[:, 0, :] = rounded[half * g : (half + 1) * g]
            tile[:, 1, :] = rounded[(2 + half) * g : (3 + half) * g]
            copy = pltpu.make_async_copy(tile, outs[half].at[:, :, columns], sem)
            copy.start()
            copies.append(copy)
    for copy in copies:
        copy.wait()


def run_parts(parts, rows, cols, lefts, like, outs=None):
    g = like.shape[0]
    fresh = outs is None
    finishing = sum(p.finish for p in parts)
    vmem, hbm = pl.BlockSpec(memory_space=pltpu.VMEM), pl.BlockSpec(memory_space=pl.ANY)
    arrays = list({id(t[2]): t[2] for p in parts for t in p.terms}.values())
    index = {id(a): i for i, a in enumerate(arrays)}
    depth, width = arrays[0].shape[1:]
    operands = [*lefts, *arrays, *(p.begun for p in parts if p.begun is not None)]
    in_specs = [vmem] * len(operands)
    out_shape, out_specs, scratch, aliases = [], [], [], {}
    if finishing:
        if not fresh:
            aliases = {len(operands): 0, len(operands) + 1: 1}
            operands, in_specs = [*operands, *outs], [*in_specs, hbm, hbm]
        out_shape, out_specs = [jax.ShapeDtypeStruct(like.shape, like.dtype)] * 2, [hbm, hbm]
        scratch = [pltpu.VMEM((g, 2, width), like.dtype), pltpu.SemaphoreType.DMA] * 2 * finishing
    sums = len(parts) - finishing
    out_shape += [jax.ShapeDtypeStruct((4 * g, width), jnp.float32)] * sums
    out_specs += [vmem] * sums
    count = sum(len(p.terms) for p in parts)
    plan = [(p.stage, [(h, m, index[id(a)], n) for h, m, a, n in p.terms], p.begun is not None, p.finish) for p in parts]
    result = pl.pallas_call(
        functools.partial(parts_kernel, plan, rows, cols, len(arrays), 2 if finishing else 0, fresh),
        out_shape=out_shape,
        in_specs=in_specs,
        out_specs=out_specs,
        scratch_shapes=scratch,
        input_output_aliases=aliases,
        compiler_params=pltpu.CompilerParams(vmem_limit_bytes=28 * 2**20),
        cost_estimate=pl.CostEstimate(flops=2 * 8 * g * depth * width * count, bytes_accessed=2**20 * count, transcendentals=0),
    )(*operands)
    return (tuple(result[:2]), result[2:]) if finishing else (outs, result)


def shards(rows, cols, orbitals, applied, ritz):
    moves = Moves(rows, cols)
    chips = rows // 2
    ahead, back = chips // 2, (chips - 1) // 2
    hops = [*range(ahead + 1), *(-h for h in range(1, back + 1))]
    lefts = [x.reshape(x.shape[0], -1) for x in (orbitals, applied)]
    run = functools.partial(run_parts, rows=rows, cols=cols, lefts=lefts, like=orbitals)

    final = cols + chips - 3
    distances = [*range(cols - 1), -1]
    mine, theirs = {(0, 0): (ritz, 0)}, {}

    def bundle(keys, gate):
        values = [lax.slice_in_dim(a, 2 * n, 2 * n + 2) if a.shape[0] > 2 else a for a, n in (mine[key] for key in keys)]
        if gate:
            values = [after(v, *gate) for v in values]
        return jnp.concatenate(values, 0) if len(values) > 1 else values[0]

    def move(how, into, sources, keys, gate, name):
        if not keys:
            return ()
        with jax.named_scope(name):
            value = how(bundle(sources, gate))
        into.update({key: (value, number) for number, key in enumerate(keys)})
        return (value,)

    def part(layer, hops, begun=None, finish=True):
        return Part(layer, [(h, whose is mine, *whose[layer, h]) for whose in (mine, theirs) for h in hops], begun, finish)

    def complete(layer):
        return [*range(chips - 1), -1] if layer in (0, -1) else [*range(chips)]

    state = {"outs": None}
    sums, used = {}, {d: [] for d in distances}

    def products(keys):
        parts = []
        for d in distances:
            hops = [h for h in complete(d) if (d, h) in keys and h not in used[d]]
            if hops:
                used[d] += hops
                parts.append(part(d, hops, sums.pop(d, None), len(used[d]) == len(complete(d))))
        parts.sort(key=lambda p: p.finish)
        state["outs"], kept = run(parts, outs=state["outs"])
        unfinished = [p for p in parts if not p.finish]
        sums.update({p.stage: s for p, s in zip(unfinished, kept, strict=True)})
        return kept[0] if unfinished else state["outs"][0]

    def tiny(value, number):
        at = 16 * (number % (ritz.shape[1] // 16))
        with jax.named_scope("token"):
            return moves.other(after(lax.slice(ritz, (0, at, 0), (1, at + 16, 128)), value))

    along_gate = gate = ()
    fresh = [(0, 0)]
    for r in range(1, final + 1):
        if r < cols - 1:
            layer, hop, step = r, 0, 1
        else:
            layer, hop, step = -1, r - (cols - 1), -1
        source = (layer - step, hop)
        z = move(lambda v: moves.along(v, step), mine, [source], [(layer, hop)], along_gate, f"along{layer}_{hop}")
        ring = [(d, r - d) for d in range(cols - 1) if 1 <= r - d <= (chips - 2 if d == 0 else chips - 1)]
        p = move(lambda v: moves.ring(v, 1), mine, [(d, h - 1) for d, h in ring], ring, gate, f"ring{r}")
        back = {1: [(0, -1)], final: [(-1, -1)]}.get(r, [])
        m = move(lambda v: moves.ring(v, -1), mine, [(d, 0) for d, _ in back], back, gate, f"back{r}")
        e = move(moves.other, theirs, fresh, fresh, gate, f"core{r}")
        fresh_before, fresh = fresh, [*ring, (layer, hop), *back]
        token = ()
        held = set(theirs) - set(fresh_before)
        if r >= chips:
            ran = products(held)
            if r == final:
                ran = products(set(theirs))
            token = (tiny(ran, r),)
        along_gate = (*p, *m, *e, *token, *(lefts if r == 1 else ()))
        gate = (*along_gate, *z)
    for key in [key for key in fresh if key != (layer, hop)]:
        move(moves.other, theirs, [key], [key], token, f"core_last{key[0]}_{key[1]}")
    products(set(theirs))
    move(moves.other, theirs, [(layer, hop)], [(layer, hop)], (), "core_end")
    products(set(theirs))
    return state["outs"]


def solution(mesh):
    rows, cols = mesh.shape["row"], mesh.shape["col"]
    whole = P(AXES, None, None)
    return jax.shard_map(
        functools.partial(shards, rows, cols),
        mesh=mesh,
        in_specs=(whole, whole, P(None, "row", "col")),
        out_specs=(whole, whole),
        check_vma=False,
    )
```

```python
import functools

import jax
import jax.numpy as jnp
from jax import lax
from jax.experimental import pallas as pl
from jax.experimental.pallas import tpu as pltpu
from jax.sharding import PartitionSpec as P

AXES = ("row", "col")


def chip_at(place, chips):
    place = place % chips
    return 2 * place if 2 * place < chips else 2 * (chips - 1 - place) + 1


class Moves:
    def __init__(self, rows, cols):
        self.chips, self.cols = rows // 2, cols

    def every(self):
        for place in range(self.chips):
            for core in range(2):
                for layer in range(self.cols):
                    yield place, core, layer

    def device(self, place, core, layer):
        return (chip_at(place, self.chips) * 2 + core) * self.cols + layer % self.cols

    def ring(self, value, step):
        pairs = [(self.device(p, k, z), self.device(p + (step if k == 0 else -step), k, z)) for p, k, z in self.every()]
        return lax.ppermute(value, AXES, pairs)

    def along(self, value, step):
        pairs = [(self.device(p, k, z), self.device(p, k, z + step)) for p, k, z in self.every()]
        return lax.ppermute(value, AXES, pairs)

    def other(self, value):
        pairs = [(self.device(p, k, z), self.device(p, 1 - k, z)) for p, k, z in self.every()]
        return lax.ppermute(value, AXES, pairs)


def after(value, *earlier):
    return lax.optimization_barrier((value,) + earlier)[0]


class Part:
    def __init__(self, stage, terms, begun=None, finish=True):
        self.stage, self.terms, self.begun, self.finish = stage, terms, begun, finish


def parts_kernel(plan, rows, cols, n_arrays, n_outs, fresh, first, second, *refs):
    refs = list(refs)
    arrays = [refs.pop(0) for _ in range(n_arrays)]
    begun = [refs.pop(0) if has else None for _, _, has, _ in plan]
    if n_outs and not fresh:
        del refs[:2]
    outs = [refs.pop(0) for _ in range(n_outs)]
    sums = [None if finish else refs.pop(0) for _, _, _, finish in plan]
    chips = rows // 2
    depth, width = arrays[0].shape[1:]
    g, bands = first.shape[0], first.shape[1] // 2
    row, layer = lax.axis_index("row"), lax.axis_index("col")
    chip, core = row // 2, row % 2
    place = jnp.where(chip % 2 == 0, chip // 2, chips - 1 - chip // 2)
    copies = []
    for i, (stage, terms, _, finish) in enumerate(plan):
        total = jnp.zeros((4 * g, width), jnp.float32) if begun[i] is None else begun[i][...]
        for hop, mine, array, number in terms:
            owner_core = core if mine else 1 - core
            at = (place + chips + jnp.where(owner_core == 0, -hop, hop)) % chips
            owner = jnp.where(2 * at < chips, 2 * at, 2 * (chips - 1 - at) + 1) * 2 + owner_core
            real = pl.ds(pl.multiple_of(owner * depth, depth), depth)
            imag = pl.ds(pl.multiple_of(bands + owner * depth, depth), depth)
            left = [jnp.concatenate([x[:, real], -x[:, imag]], 1) for x in (first, second)]
            left += [jnp.concatenate([x[:, imag], x[:, real]], 1) for x in (first, second)]
            right = arrays[array][2 * number : 2 * number + 2].reshape(2 * depth, width)
            total += jnp.dot(jnp.concatenate(left, 0), right, preferred_element_type=jnp.float32)
        if not finish:
            sums[i][...] = total
            continue
        rounded = total.astype(outs[0].dtype)
        columns = pl.ds(pl.multiple_of(((layer + cols - stage) % cols) * width, width), width)
        for half in range(2):
            tile, sem = refs.pop(0), refs.pop(0)
            tile[:, 0, :] = rounded[half * g : (half + 1) * g]
            tile[:, 1, :] = rounded[(2 + half) * g : (3 + half) * g]
            copy = pltpu.make_async_copy(tile, outs[half].at[:, :, columns], sem)
            copy.start()
            copies.append(copy)
    for copy in copies:
        copy.wait()


def run_parts(parts, rows, cols, lefts, like, outs=None):
    g = like.shape[0]
    fresh = outs is None
    finishing = sum(p.finish for p in parts)
    vmem, hbm = pl.BlockSpec(memory_space=pltpu.VMEM), pl.BlockSpec(memory_space=pl.ANY)
    arrays = list({id(t[2]): t[2] for p in parts for t in p.terms}.values())
    index = {id(a): i for i, a in enumerate(arrays)}
    depth, width = arrays[0].shape[1:]
    operands = [*lefts, *arrays, *(p.begun for p in parts if p.begun is not None)]
    in_specs = [vmem] * len(operands)
    out_shape, out_specs, scratch, aliases = [], [], [], {}
    if finishing:
        if not fresh:
            aliases = {len(operands): 0, len(operands) + 1: 1}
            operands, in_specs = [*operands, *outs], [*in_specs, hbm, hbm]
        out_shape, out_specs = [jax.ShapeDtypeStruct(like.shape, like.dtype)] * 2, [hbm, hbm]
        scratch = [pltpu.VMEM((g, 2, width), like.dtype), pltpu.SemaphoreType.DMA] * 2 * finishing
    sums = len(parts) - finishing
    out_shape += [jax.ShapeDtypeStruct((4 * g, width), jnp.float32)] * sums
    out_specs += [vmem] * sums
    count = sum(len(p.terms) for p in parts)
    plan = [(p.stage, [(h, m, index[id(a)], n) for h, m, a, n in p.terms], p.begun is not None, p.finish) for p in parts]
    result = pl.pallas_call(
        functools.partial(parts_kernel, plan, rows, cols, len(arrays), 2 if finishing else 0, fresh),
        out_shape=out_shape,
        in_specs=in_specs,
        out_specs=out_specs,
        scratch_shapes=scratch,
        input_output_aliases=aliases,
        compiler_params=pltpu.CompilerParams(vmem_limit_bytes=28 * 2**20),
        cost_estimate=pl.CostEstimate(flops=2 * 8 * g * depth * width * count, bytes_accessed=2**20 * count, transcendentals=0),
    )(*operands)
    return (tuple(result[:2]), result[2:]) if finishing else (outs, result)


def few_rounds(moves, run, lefts, ritz):
    distances = [0, 1, 2, -1]
    mine, theirs = {(0, 0): (ritz, 0)}, {}
    full = {0: [0, 1, 2, -1], 1: [0, 1, 2, -1], 2: [0, 1, 2, -1], -1: [0, 1, 2, -1]}

    def bundle(keys, gate):
        values = [lax.slice_in_dim(a, 2 * n, 2 * n + 2) if a.shape[0] > 2 else a for a, n in (mine[key] for key in keys)]
        values = [after(v, *gate) for v in values]
        return jnp.concatenate(values, 0) if len(values) > 1 else values[0]

    def move(how, step, pairs, *gate):
        with jax.named_scope(how + "_".join(f"{d}:{h}" for _, (d, h) in pairs)):
            value = getattr(moves, how)(bundle([source for source, _ in pairs], gate), step)
        mine.update({key: (value, number) for number, (_, key) in enumerate(pairs)})
        return value

    def swap(keys, *gate):
        with jax.named_scope("core" + "_".join(f"{d}:{h}" for d, h in keys)):
            value = moves.other(bundle(keys, gate))
        theirs.update({key: (value, number) for number, key in enumerate(keys)})
        return value

    def part(layer, hops, begun=None, finish=True):
        return Part(layer, [(h, whose is mine, *whose[layer, h]) for whose in (mine, theirs) for h in hops], begun, finish)

    state = {"outs": None, "tokens": 0}
    sums, used = {}, {d: [] for d in distances}

    def products(keys):
        parts = []
        for d in distances:
            hops = [h for h in full[d] if (d, h) in keys and h not in used[d]]
            if hops:
                used[d] += hops
                parts.append(part(d, hops, sums.pop(d, None), len(used[d]) == len(full[d])))
        parts.sort(key=lambda p: p.finish)
        state["outs"], kept = run(parts, outs=state["outs"])
        unfinished = [p for p in parts if not p.finish]
        sums.update({p.stage: s for p, s in zip(unfinished, kept, strict=True)})
        return kept[0] if unfinished else state["outs"][0]

    def token(value):
        at = 16 * state["tokens"]
        state["tokens"] += 1
        with jax.named_scope("token"):
            return moves.other(after(lax.slice(ritz, (0, at, 0), (1, at + 16, 128)), value))

    cut = ritz.shape[1] // 2

    def down(value, name, *gate):
        with jax.named_scope(name):
            return moves.along(after(value, *gate), -1)

    z1 = move("along", 1, [((0, 0), (1, 0))])
    p1 = move("ring", 1, [((0, 0), (0, 1))])
    m1 = move("ring", -1, [((0, 0), (0, -1))])
    e1 = swap([(0, 0)])
    gate = (p1, m1, z1, e1, *lefts)
    z2 = move("along", 1, [((1, 0), (2, 0))], *gate)
    p2 = move("ring", 1, [((0, 1), (0, 2)), ((1, 0), (1, 1))], *gate)
    m2 = move("ring", -1, [((1, 0), (1, -1))], *gate)
    upper = down(ritz[:, :cut], "along_upper", *gate)
    e2 = swap([(0, 1), (0, -1), (1, 0)], *gate)
    gate = (p2, m2, e2, z2, upper)
    p3 = move("ring", 1, [((1, 1), (1, 2)), ((2, 0), (2, 1))], *gate)
    m3 = move("ring", -1, [((2, 0), (2, -1))], *gate)
    lower = down(jnp.concatenate([ritz[:, cut:], mine[0, 1][0]], 1), "along_lower", *gate)
    e3 = swap([(0, 2), (1, 1), (1, -1), (2, 0)], *gate)
    products([(0, 0), (0, 1), (0, -1), (1, 0)])
    t = token(products([(0, 2), (1, 1), (1, -1), (2, 0)]))
    mine[-1, 0] = jnp.concatenate([upper, lower[:, : ritz.shape[1] - cut]], 1), 0
    mine[-1, 1] = lower[:, ritz.shape[1] - cut :], 0
    gate = (p3, m3, e3, t)
    z5 = move("along", -1, [((0, 2), (-1, 2))], *gate)
    gate = (*gate, lower)
    p4 = move("ring", 1, [((2, 1), (2, 2))], *gate)
    m4 = move("ring", -1, [((-1, 0), (-1, -1))], *gate)
    e4 = swap([(1, 2), (2, 1), (2, -1)], *gate)
    e4b = swap([(-1, 0), (-1, 1)], *gate)
    t = token(products([(1, 2), (2, 1), (2, -1), (-1, 0), (-1, 1)]))
    swap([(2, 2)], t, e4)
    swap([(-1, -1)], t, e4)
    products([(2, 2), (-1, -1)])
    swap([(-1, 2)])
    products([(-1, 2)])
    return state["outs"]


def any_rounds(moves, run, lefts, ritz):
    chips, cols = moves.chips, moves.cols
    final = cols + chips - 3
    distances = [*range(cols - 1), -1]
    mine, theirs = {(0, 0): (ritz, 0)}, {}

    def bundle(keys, gate):
        values = [lax.slice_in_dim(a, 2 * n, 2 * n + 2) if a.shape[0] > 2 else a for a, n in (mine[key] for key in keys)]
        if gate:
            values = [after(v, *gate) for v in values]
        return jnp.concatenate(values, 0) if len(values) > 1 else values[0]

    def move(how, into, sources, keys, gate, name):
        if not keys:
            return ()
        with jax.named_scope(name):
            value = how(bundle(sources, gate))
        into.update({key: (value, number) for number, key in enumerate(keys)})
        return (value,)

    def part(layer, hops, begun=None, finish=True):
        return Part(layer, [(h, whose is mine, *whose[layer, h]) for whose in (mine, theirs) for h in hops], begun, finish)

    def complete(layer):
        return [*range(chips - 1), -1] if layer in (0, -1) else [*range(chips)]

    state = {"outs": None}
    sums, used = {}, {d: [] for d in distances}

    def products(keys):
        parts = []
        for d in distances:
            hops = [h for h in complete(d) if (d, h) in keys and h not in used[d]]
            if hops:
                used[d] += hops
                parts.append(part(d, hops, sums.pop(d, None), len(used[d]) == len(complete(d))))
        parts.sort(key=lambda p: p.finish)
        state["outs"], kept = run(parts, outs=state["outs"])
        unfinished = [p for p in parts if not p.finish]
        sums.update({p.stage: s for p, s in zip(unfinished, kept, strict=True)})
        return kept[0] if unfinished else state["outs"][0]

    def tiny(value, number):
        at = 16 * (number % (ritz.shape[1] // 16))
        with jax.named_scope("token"):
            return moves.other(after(lax.slice(ritz, (0, at, 0), (1, at + 16, 128)), value))

    along_gate = gate = ()
    fresh = [(0, 0)]
    for r in range(1, final + 1):
        if r < cols - 1:
            layer, hop, step = r, 0, 1
        else:
            layer, hop, step = -1, r - (cols - 1), -1
        source = (layer - step, hop)
        z = move(lambda v: moves.along(v, step), mine, [source], [(layer, hop)], along_gate, f"along{layer}_{hop}")
        ring = [(d, r - d) for d in range(cols - 1) if 1 <= r - d <= (chips - 2 if d == 0 else chips - 1)]
        p = move(lambda v: moves.ring(v, 1), mine, [(d, h - 1) for d, h in ring], ring, gate, f"ring{r}")
        back = {1: [(0, -1)], final: [(-1, -1)]}.get(r, [])
        m = move(lambda v: moves.ring(v, -1), mine, [(d, 0) for d, _ in back], back, gate, f"back{r}")
        e = move(moves.other, theirs, fresh, fresh, gate, f"core{r}")
        fresh_before, fresh = fresh, [*ring, (layer, hop), *back]
        token = ()
        held = set(theirs) - set(fresh_before)
        if r >= chips:
            ran = products(held)
            if r == final:
                ran = products(set(theirs))
            token = (tiny(ran, r),)
        along_gate = (*p, *m, *e, *token, *(lefts if r == 1 else ()))
        gate = (*along_gate, *z)
    for key in [key for key in fresh if key != (layer, hop)]:
        move(moves.other, theirs, [key], [key], token, f"core_last{key[0]}_{key[1]}")
    products(set(theirs))
    move(moves.other, theirs, [(layer, hop)], [(layer, hop)], (), "core_end")
    products(set(theirs))
    return state["outs"]


def shards(rows, cols, orbitals, applied, ritz):
    moves = Moves(rows, cols)
    lefts = [x.reshape(x.shape[0], -1) for x in (orbitals, applied)]
    run = functools.partial(run_parts, rows=rows, cols=cols, lefts=lefts, like=orbitals)
    return (few_rounds if (moves.chips, cols) == (4, 4) else any_rounds)(moves, run, lefts, ritz)


def solution(mesh):
    rows, cols = mesh.shape["row"], mesh.shape["col"]
    whole = P(AXES, None, None)
    return jax.shard_map(
        functools.partial(shards, rows, cols),
        mesh=mesh,
        in_specs=(whole, whole, P(None, "row", "col")),
        out_specs=(whole, whole),
        check_vma=False,
    )
```

```python
import functools

import jax
import jax.numpy as jnp
from jax import lax
from jax.experimental import pallas as pl
from jax.experimental.pallas import tpu as pltpu
from jax.sharding import PartitionSpec as P

AXES = ("row", "col")


def chip_at(place, chips):
    place = place % chips
    return 2 * place if 2 * place < chips else 2 * (chips - 1 - place) + 1


class Moves:
    def __init__(self, rows, cols):
        self.chips, self.cols = rows // 2, cols

    def every(self):
        for place in range(self.chips):
            for core in range(2):
                for layer in range(self.cols):
                    yield place, core, layer

    def device(self, place, core, layer):
        return (chip_at(place, self.chips) * 2 + core) * self.cols + layer % self.cols

    def ring(self, value, step):
        pairs = [(self.device(p, k, z), self.device(p + (step if k == 0 else -step), k, z)) for p, k, z in self.every()]
        return lax.ppermute(value, AXES, pairs)

    def along(self, value, step):
        pairs = [(self.device(p, k, z), self.device(p, k, z + step)) for p, k, z in self.every()]
        return lax.ppermute(value, AXES, pairs)

    def other(self, value):
        pairs = [(self.device(p, k, z), self.device(p, 1 - k, z)) for p, k, z in self.every()]
        return lax.ppermute(value, AXES, pairs)


def after(value, *earlier):
    return lax.optimization_barrier((value,) + earlier)[0]


class Part:
    def __init__(self, stage, terms, begun=(), finish=True):
        self.stage, self.terms, self.begun, self.finish = stage, terms, begun, finish


def parts_kernel(plan, rows, cols, n_arrays, n_outs, fresh, first, second, *refs):
    refs = list(refs)
    arrays = [refs.pop(0) for _ in range(n_arrays)]
    begun = [[refs.pop(0) for _ in range(count)] for _, _, count, _ in plan]
    if n_outs and not fresh:
        del refs[:2]
    outs = [refs.pop(0) for _ in range(n_outs)]
    sums = [None if finish else refs.pop(0) for _, _, _, finish in plan]
    chips = rows // 2
    depth, width = arrays[0].shape[1:]
    g, bands = first.shape[0], first.shape[1] // 2
    row, layer = lax.axis_index("row"), lax.axis_index("col")
    chip, core = row // 2, row % 2
    place = jnp.where(chip % 2 == 0, chip // 2, chips - 1 - chip // 2)
    copies = []
    for i, (stage, terms, _, finish) in enumerate(plan):
        total = jnp.zeros((4 * g, width), jnp.float32) if not begun[i] else functools.reduce(jnp.add, [b[...] for b in begun[i]])
        for hop, mine, array, number in terms:
            owner_core = core if mine else 1 - core
            at = (place + chips + jnp.where(owner_core == 0, -hop, hop)) % chips
            owner = jnp.where(2 * at < chips, 2 * at, 2 * (chips - 1 - at) + 1) * 2 + owner_core
            real = pl.ds(pl.multiple_of(owner * depth, depth), depth)
            imag = pl.ds(pl.multiple_of(bands + owner * depth, depth), depth)
            left = [jnp.concatenate([x[:, real], -x[:, imag]], 1) for x in (first, second)]
            left += [jnp.concatenate([x[:, imag], x[:, real]], 1) for x in (first, second)]
            right = arrays[array][2 * number : 2 * number + 2].reshape(2 * depth, width)
            total += jnp.dot(jnp.concatenate(left, 0), right, preferred_element_type=jnp.float32)
        if not finish:
            sums[i][...] = total
            continue
        rounded = total.astype(outs[0].dtype)
        columns = pl.ds(pl.multiple_of(((layer + cols - stage) % cols) * width, width), width)
        for half in range(2):
            tile, sem = refs.pop(0), refs.pop(0)
            tile[:, 0, :] = rounded[half * g : (half + 1) * g]
            tile[:, 1, :] = rounded[(2 + half) * g : (3 + half) * g]
            copy = pltpu.make_async_copy(tile, outs[half].at[:, :, columns], sem)
            copy.start()
            copies.append(copy)
    for copy in copies:
        copy.wait()


def run_parts(parts, rows, cols, lefts, like, outs=None, weight=1):
    g = like.shape[0]
    fresh = outs is None
    finishing = sum(p.finish for p in parts)
    vmem, hbm = pl.BlockSpec(memory_space=pltpu.VMEM), pl.BlockSpec(memory_space=pl.ANY)
    arrays = list({id(t[2]): t[2] for p in parts for t in p.terms}.values())
    index = {id(a): i for i, a in enumerate(arrays)}
    depth, width = arrays[0].shape[1:]
    operands = [*lefts, *arrays, *(b for p in parts for b in p.begun)]
    in_specs = [vmem] * len(operands)
    out_shape, out_specs, scratch, aliases = [], [], [], {}
    if finishing:
        if not fresh:
            aliases = {len(operands): 0, len(operands) + 1: 1}
            operands, in_specs = [*operands, *outs], [*in_specs, hbm, hbm]
        out_shape, out_specs = [jax.ShapeDtypeStruct(like.shape, like.dtype)] * 2, [hbm, hbm]
        scratch = [pltpu.VMEM((g, 2, width), like.dtype), pltpu.SemaphoreType.DMA] * 2 * finishing
    sums = len(parts) - finishing
    out_shape += [jax.ShapeDtypeStruct((4 * g, width), jnp.float32)] * sums
    out_specs += [vmem] * sums
    count = sum(len(p.terms) for p in parts)
    plan = [(p.stage, [(h, m, index[id(a)], n) for h, m, a, n in p.terms], len(p.begun), p.finish) for p in parts]
    result = pl.pallas_call(
        functools.partial(parts_kernel, plan, rows, cols, len(arrays), 2 if finishing else 0, fresh),
        out_shape=out_shape,
        in_specs=in_specs,
        out_specs=out_specs,
        scratch_shapes=scratch,
        input_output_aliases=aliases,
        compiler_params=pltpu.CompilerParams(vmem_limit_bytes=28 * 2**20),
        cost_estimate=pl.CostEstimate(flops=weight * 2 * 8 * g * depth * width * count, bytes_accessed=2**20 * count, transcendentals=0),
    )(*operands)
    return (tuple(result[:2]), result[2:]) if finishing else (outs, result)


def few_rounds(moves, run, lefts, ritz):
    distances = [0, 1, 2, -1]
    mine, theirs = {(0, 0): (ritz, 0)}, {}
    full = {0: [0, 1, 2, -1], 1: [0, 1, 2, -1], 2: [0, 1, 2, -1], -1: [0, 1, 2, -1]}

    def bundle(keys, gate):
        values = [lax.slice_in_dim(a, 2 * n, 2 * n + 2) if a.shape[0] > 2 else a for a, n in (mine[key] for key in keys)]
        values = [after(v, *gate) for v in values]
        return jnp.concatenate(values, 0) if len(values) > 1 else values[0]

    def move(how, step, pairs, *gate):
        with jax.named_scope(how + "_".join(f"{d}:{h}" for _, (d, h) in pairs)):
            value = getattr(moves, how)(bundle([source for source, _ in pairs], gate), step)
        mine.update({key: (value, number) for number, (_, key) in enumerate(pairs)})
        return value

    def swap(keys, *gate):
        with jax.named_scope("core" + "_".join(f"{d}:{h}" for d, h in keys)):
            value = moves.other(bundle(keys, gate))
        theirs.update({key: (value, number) for number, key in enumerate(keys)})
        return value

    state = {"outs": None, "tokens": 0}
    sums, used = {d: [] for d in distances}, {d: [] for d in distances}

    def products(who, keys, fresh=(), more=(), weight=1):
        parts = []
        for d in distances:
            terms = [(h, whose is mine, *whose[d, h]) for whose in who for e, h in keys if e == d]
            terms += [(h, whose is mine, *whose[d, h]) for whose, e, h in more if e == d]
            if terms:
                used[d] += terms
                begun = []
                if d not in fresh:
                    begun, sums[d] = sums[d], []
                parts.append(Part(d, terms, begun, d not in fresh and len(used[d]) == 2 * len(full[d])))
        parts.sort(key=lambda p: p.finish)
        state["outs"], kept = run(parts, outs=state["outs"], weight=weight)
        unfinished = [p for p in parts if not p.finish]
        for p, s in zip(unfinished, kept, strict=True):
            sums[p.stage].append(s)
        return kept[0] if unfinished else state["outs"][0]

    def token(value):
        at = 16 * state["tokens"]
        state["tokens"] += 1
        with jax.named_scope("token"):
            return moves.other(after(lax.slice(ritz, (0, at, 0), (1, at + 16, 128)), value))

    both = (mine, theirs)
    cut = ritz.shape[1] // 2

    def down(value, name, *gate):
        with jax.named_scope(name):
            return moves.along(after(value, *gate), -1)

    z1 = move("along", 1, [((0, 0), (1, 0))])
    p1 = move("ring", 1, [((0, 0), (0, 1))])
    m1 = move("ring", -1, [((0, 0), (0, -1))], *lefts)
    e1 = swap([(0, 0)], *lefts)
    x2 = move("ring", 1, [((0, 1), (0, 2))], *lefts)
    gate = (p1, z1)
    z2 = move("along", 1, [((1, 0), (2, 0))], *gate)
    s1 = move("ring", 1, [((1, 0), (1, 1))], *gate)
    m2 = move("ring", -1, [((1, 0), (1, -1))], m1, *gate)
    upper = down(ritz[:, :cut], "along_upper", m1, *gate)
    gate = (lax.slice(x2, (0, 0, 0), (1, 16, 128)), s1, m2, e1, z2, upper)
    p3 = move("ring", 1, [((1, 1), (1, 2)), ((2, 0), (2, 1))], *gate)
    m3 = move("ring", -1, [((2, 0), (2, -1))], *gate)
    lower = down(jnp.concatenate([ritz[:, cut:], mine[0, 1][0]], 1), "along_lower", *gate)
    e3 = swap([(0, 1), (0, -1), (0, 2), (1, 0)], *gate)
    e3b = swap([(1, 1), (1, -1), (2, 0)], *gate)
    products(both, [(0, 0), (0, 1), (0, -1), (0, 2), (1, 0)])
    t = token(products(both, [(1, 1), (1, -1), (2, 0)]))
    mine[-1, 0] = jnp.concatenate([upper, lower[:, : ritz.shape[1] - cut]], 1), 0
    mine[-1, 1] = lower[:, ritz.shape[1] - cut :], 0
    gate = (p3, m3, e3, t)
    z5 = move("along", -1, [((0, 2), (-1, 2))], *gate)
    gate = (*gate, lower)
    p4 = move("ring", 1, [((2, 1), (2, 2))], *gate)
    m4 = move("ring", -1, [((-1, 0), (-1, -1))], *gate)
    e4 = swap([(1, 2), (2, 1), (2, -1)], *gate)
    e4b = swap([(-1, 0), (-1, 1)], *gate)
    t = token(products(both, [(1, 2), (2, 1), (2, -1), (-1, 0), (-1, 1)]))
    swap([(2, 2)], t, e4)
    swap([(-1, -1)], t, e4)
    swap([(-1, 2)], t, e4)
    products([mine], [(2, 2), (-1, -1), (-1, 2)], (2, -1))
    products([theirs], [(2, 2)])
    products([theirs], [(-1, -1), (-1, 2)])
    return state["outs"]


def any_rounds(moves, run, lefts, ritz):
    chips, cols = moves.chips, moves.cols
    final = cols + chips - 3
    distances = [*range(cols - 1), -1]
    mine, theirs = {(0, 0): (ritz, 0)}, {}

    def bundle(keys, gate):
        values = [lax.slice_in_dim(a, 2 * n, 2 * n + 2) if a.shape[0] > 2 else a for a, n in (mine[key] for key in keys)]
        if gate:
            values = [after(v, *gate) for v in values]
        return jnp.concatenate(values, 0) if len(values) > 1 else values[0]

    def move(how, into, sources, keys, gate, name):
        if not keys:
            return ()
        with jax.named_scope(name):
            value = how(bundle(sources, gate))
        into.update({key: (value, number) for number, key in enumerate(keys)})
        return (value,)

    def part(layer, hops, begun=None, finish=True):
        return Part(layer, [(h, whose is mine, *whose[layer, h]) for whose in (mine, theirs) for h in hops], () if begun is None else (begun,), finish)

    def complete(layer):
        return [*range(chips - 1), -1] if layer in (0, -1) else [*range(chips)]

    state = {"outs": None}
    sums, used = {}, {d: [] for d in distances}

    def products(keys):
        parts = []
        for d in distances:
            hops = [h for h in complete(d) if (d, h) in keys and h not in used[d]]
            if hops:
                used[d] += hops
                parts.append(part(d, hops, sums.pop(d, None), len(used[d]) == len(complete(d))))
        parts.sort(key=lambda p: p.finish)
        state["outs"], kept = run(parts, outs=state["outs"])
        unfinished = [p for p in parts if not p.finish]
        sums.update({p.stage: s for p, s in zip(unfinished, kept, strict=True)})
        return kept[0] if unfinished else state["outs"][0]

    def tiny(value, number):
        at = 16 * (number % (ritz.shape[1] // 16))
        with jax.named_scope("token"):
            return moves.other(after(lax.slice(ritz, (0, at, 0), (1, at + 16, 128)), value))

    along_gate = gate = ()
    fresh = [(0, 0)]
    for r in range(1, final + 1):
        if r < cols - 1:
            layer, hop, step = r, 0, 1
        else:
            layer, hop, step = -1, r - (cols - 1), -1
        source = (layer - step, hop)
        z = move(lambda v: moves.along(v, step), mine, [source], [(layer, hop)], along_gate, f"along{layer}_{hop}")
        ring = [(d, r - d) for d in range(cols - 1) if 1 <= r - d <= (chips - 2 if d == 0 else chips - 1)]
        p = move(lambda v: moves.ring(v, 1), mine, [(d, h - 1) for d, h in ring], ring, gate, f"ring{r}")
        back = {1: [(0, -1)], final: [(-1, -1)]}.get(r, [])
        m = move(lambda v: moves.ring(v, -1), mine, [(d, 0) for d, _ in back], back, gate, f"back{r}")
        e = move(moves.other, theirs, fresh, fresh, gate, f"core{r}")
        fresh_before, fresh = fresh, [*ring, (layer, hop), *back]
        token = ()
        held = set(theirs) - set(fresh_before)
        if r >= chips:
            ran = products(held)
            if r == final:
                ran = products(set(theirs))
            token = (tiny(ran, r),)
        along_gate = (*p, *m, *e, *token, *(lefts if r == 1 else ()))
        gate = (*along_gate, *z)
    for key in [key for key in fresh if key != (layer, hop)]:
        move(moves.other, theirs, [key], [key], token, f"core_last{key[0]}_{key[1]}")
    products(set(theirs))
    move(moves.other, theirs, [(layer, hop)], [(layer, hop)], (), "core_end")
    products(set(theirs))
    return state["outs"]


def shards(rows, cols, orbitals, applied, ritz):
    moves = Moves(rows, cols)
    lefts = [x.reshape(x.shape[0], -1) for x in (orbitals, applied)]
    run = functools.partial(run_parts, rows=rows, cols=cols, lefts=lefts, like=orbitals)
    return (few_rounds if (moves.chips, cols) == (4, 4) else any_rounds)(moves, run, lefts, ritz)


def solution(mesh):
    rows, cols = mesh.shape["row"], mesh.shape["col"]
    whole = P(AXES, None, None)
    return jax.shard_map(
        functools.partial(shards, rows, cols),
        mesh=mesh,
        in_specs=(whole, whole, P(None, "row", "col")),
        out_specs=(whole, whole),
        check_vma=False,
    )
```

```python
import functools

import jax
import jax.numpy as jnp
from jax import lax
from jax.experimental import pallas as pl
from jax.experimental.pallas import tpu as pltpu
from jax.sharding import PartitionSpec as P

AXES = ("row", "col")


def chip_at(place, chips):
    place = place % chips
    return 2 * place if 2 * place < chips else 2 * (chips - 1 - place) + 1


class Moves:
    def __init__(self, rows, cols):
        self.chips, self.cols = rows // 2, cols

    def every(self):
        for place in range(self.chips):
            for core in range(2):
                for layer in range(self.cols):
                    yield place, core, layer

    def device(self, place, core, layer):
        return (chip_at(place, self.chips) * 2 + core) * self.cols + layer % self.cols

    def ring(self, value, step):
        pairs = [(self.device(p, k, z), self.device(p + (step if k == 0 else -step), k, z)) for p, k, z in self.every()]
        return lax.ppermute(value, AXES, pairs)

    def along(self, value, step):
        pairs = [(self.device(p, k, z), self.device(p, k, z + step)) for p, k, z in self.every()]
        return lax.ppermute(value, AXES, pairs)

    def other(self, value):
        pairs = [(self.device(p, k, z), self.device(p, 1 - k, z)) for p, k, z in self.every()]
        return lax.ppermute(value, AXES, pairs)


def after(value, *earlier):
    return lax.optimization_barrier((value,) + earlier)[0]


class Part:
    def __init__(self, stage, terms, begun=(), finish=True):
        self.stage, self.terms, self.begun, self.finish = stage, terms, begun, finish


def parts_kernel(plan, rows, cols, n_arrays, n_outs, fresh, first, second, *refs):
    refs = list(refs)
    arrays = [refs.pop(0) for _ in range(n_arrays)]
    begun = [[refs.pop(0) for _ in range(count)] for _, _, count, _ in plan]
    if n_outs and not fresh:
        del refs[:2]
    outs = [refs.pop(0) for _ in range(n_outs)]
    sums = [None if finish else refs.pop(0) for _, _, _, finish in plan]
    chips = rows // 2
    depth, width = arrays[0].shape[1:]
    g, bands = first.shape[0], first.shape[1] // 2
    row, layer = lax.axis_index("row"), lax.axis_index("col")
    chip, core = row // 2, row % 2
    place = jnp.where(chip % 2 == 0, chip // 2, chips - 1 - chip // 2)
    copies = []
    for i, (stage, terms, _, finish) in enumerate(plan):
        total = jnp.zeros((4 * g, width), jnp.float32) if not begun[i] else functools.reduce(jnp.add, [b[...] for b in begun[i]])
        for hop, mine, array, number in terms:
            owner_core = core if mine else 1 - core
            at = (place + chips + jnp.where(owner_core == 0, -hop, hop)) % chips
            owner = jnp.where(2 * at < chips, 2 * at, 2 * (chips - 1 - at) + 1) * 2 + owner_core
            real = pl.ds(pl.multiple_of(owner * depth, depth), depth)
            imag = pl.ds(pl.multiple_of(bands + owner * depth, depth), depth)
            left = [jnp.concatenate([x[:, real], -x[:, imag]], 1) for x in (first, second)]
            left += [jnp.concatenate([x[:, imag], x[:, real]], 1) for x in (first, second)]
            right = arrays[array][2 * number : 2 * number + 2].reshape(2 * depth, width)
            total += jnp.dot(jnp.concatenate(left, 0), right, preferred_element_type=jnp.float32)
        if not finish:
            sums[i][...] = total
            continue
        rounded = total.astype(outs[0].dtype)
        columns = pl.ds(pl.multiple_of(((layer + cols - stage) % cols) * width, width), width)
        for half in range(2):
            tile, sem = refs.pop(0), refs.pop(0)
            tile[:, 0, :] = rounded[half * g : (half + 1) * g]
            tile[:, 1, :] = rounded[(2 + half) * g : (3 + half) * g]
            copy = pltpu.make_async_copy(tile, outs[half].at[:, :, columns], sem)
            copy.start()
            copies.append(copy)
    for copy in copies:
        copy.wait()


def run_parts(parts, rows, cols, lefts, like, outs=None, weight=1):
    g = like.shape[0]
    fresh = outs is None
    finishing = sum(p.finish for p in parts)
    vmem, hbm = pl.BlockSpec(memory_space=pltpu.VMEM), pl.BlockSpec(memory_space=pl.ANY)
    arrays = list({id(t[2]): t[2] for p in parts for t in p.terms}.values())
    index = {id(a): i for i, a in enumerate(arrays)}
    depth, width = arrays[0].shape[1:]
    operands = [*lefts, *arrays, *(b for p in parts for b in p.begun)]
    in_specs = [vmem] * len(operands)
    out_shape, out_specs, scratch, aliases = [], [], [], {}
    if finishing:
        if not fresh:
            aliases = {len(operands): 0, len(operands) + 1: 1}
            operands, in_specs = [*operands, *outs], [*in_specs, hbm, hbm]
        out_shape, out_specs = [jax.ShapeDtypeStruct(like.shape, like.dtype)] * 2, [hbm, hbm]
        scratch = [pltpu.VMEM((g, 2, width), like.dtype), pltpu.SemaphoreType.DMA] * 2 * finishing
    sums = len(parts) - finishing
    out_shape += [jax.ShapeDtypeStruct((4 * g, width), jnp.float32)] * sums
    out_specs += [vmem] * sums
    count = sum(len(p.terms) for p in parts)
    plan = [(p.stage, [(h, m, index[id(a)], n) for h, m, a, n in p.terms], len(p.begun), p.finish) for p in parts]
    result = pl.pallas_call(
        functools.partial(parts_kernel, plan, rows, cols, len(arrays), 2 if finishing else 0, fresh),
        out_shape=out_shape,
        in_specs=in_specs,
        out_specs=out_specs,
        scratch_shapes=scratch,
        input_output_aliases=aliases,
        compiler_params=pltpu.CompilerParams(vmem_limit_bytes=28 * 2**20),
        cost_estimate=pl.CostEstimate(flops=weight * 2 * 8 * g * depth * width * count, bytes_accessed=2**20 * count, transcendentals=0),
    )(*operands)
    return (tuple(result[:2]), result[2:]) if finishing else (outs, result)


def few_rounds(moves, run, lefts, ritz):
    distances = [0, 1, 2, -1]
    mine, theirs = {(0, 0): (ritz, 0)}, {}
    full = {0: [0, 1, 2, -1], 1: [0, 1, 2, -1], 2: [0, 1, 2, -1], -1: [0, 1, 2, -1]}

    def bundle(keys, gate):
        values = [lax.slice_in_dim(a, 2 * n, 2 * n + 2) if a.shape[0] > 2 else a for a, n in (mine[key] for key in keys)]
        values = [after(v, *gate) for v in values]
        return jnp.concatenate(values, 0) if len(values) > 1 else values[0]

    def move(how, step, pairs, *gate):
        with jax.named_scope(how + "_".join(f"{d}:{h}" for _, (d, h) in pairs)):
            value = getattr(moves, how)(bundle([source for source, _ in pairs], gate), step)
        mine.update({key: (value, number) for number, (_, key) in enumerate(pairs)})
        return value

    def swap(keys, *gate):
        with jax.named_scope("core" + "_".join(f"{d}:{h}" for d, h in keys)):
            value = moves.other(bundle(keys, gate))
        theirs.update({key: (value, number) for number, key in enumerate(keys)})
        return value

    state = {"outs": None, "tokens": 0}
    sums, used = {d: [] for d in distances}, {d: [] for d in distances}

    def products(who, keys, fresh=(), more=(), weight=1):
        parts = []
        for d in distances:
            terms = [(h, whose is mine, *whose[d, h]) for whose in who for e, h in keys if e == d]
            terms += [(h, whose is mine, *whose[d, h]) for whose, e, h in more if e == d]
            if terms:
                used[d] += terms
                begun = []
                if d not in fresh:
                    begun, sums[d] = sums[d], []
                parts.append(Part(d, terms, begun, d not in fresh and len(used[d]) == 2 * len(full[d])))
        parts.sort(key=lambda p: p.finish)
        state["outs"], kept = run(parts, outs=state["outs"], weight=weight)
        unfinished = [p for p in parts if not p.finish]
        for p, s in zip(unfinished, kept, strict=True):
            sums[p.stage].append(s)
        return kept[0] if unfinished else state["outs"][0]

    def token(value):
        at = 16 * state["tokens"]
        state["tokens"] += 1
        with jax.named_scope("token"):
            return moves.other(after(lax.slice(ritz, (0, at, 0), (1, at + 16, 128)), value))

    both = (mine, theirs)
    cut = ritz.shape[1] // 2

    def down(value, name, *gate):
        with jax.named_scope(name):
            return moves.along(after(value, *gate), -1)

    z1 = move("along", 1, [((0, 0), (1, 0))])
    p1 = move("ring", 1, [((0, 0), (0, 1))])
    m1 = move("ring", -1, [((0, 0), (0, -1))], *lefts)
    e1 = swap([(0, 0)], *lefts)
    x2 = move("ring", 1, [((0, 1), (0, 2))], *lefts)
    gate = (p1, z1)
    z2 = move("along", 1, [((1, 0), (2, 0))], *gate)
    s1 = move("ring", 1, [((1, 0), (1, 1))], *gate)
    m2 = move("ring", -1, [((1, 0), (1, -1))], m1, *gate)
    upper = down(ritz[:, :cut], "along_upper", m1, *gate)
    gate = (lax.slice(x2, (0, 0, 0), (1, 16, 128)), s1, m2, e1, z2, upper)
    p3 = move("ring", 1, [((1, 1), (1, 2)), ((2, 0), (2, 1))], *gate)
    m3 = move("ring", -1, [((2, 0), (2, -1))], *gate)
    lower = down(jnp.concatenate([ritz[:, cut:], mine[0, 1][0]], 1), "along_lower", *gate)
    e3 = swap([(0, 1), (0, -1), (0, 2), (1, 0)], *gate)
    e3b = swap([(1, 1), (1, -1), (2, 0)], *gate)
    products(both, [(0, 0), (0, 1), (0, -1), (0, 2), (1, 0)])
    t = token(products(both, [(1, 1), (1, -1), (2, 0)]))
    mine[-1, 0] = jnp.concatenate([upper, lower[:, : ritz.shape[1] - cut]], 1), 0
    mine[-1, 1] = lower[:, ritz.shape[1] - cut :], 0
    gate = (p3, m3, e3, t)
    z5 = move("along", -1, [((0, 2), (-1, 2))], m3, e3, t)
    gate = (*gate, lower)
    p4 = move("ring", 1, [((2, 1), (2, 2))], *gate)
    e4 = swap([(1, 2), (2, 1), (2, -1)], *gate)
    e4b = swap([(-1, 0), (-1, 1)], *gate)
    m4 = move("ring", -1, [((-1, 0), (-1, -1))], e4b, *gate)
    t = token(products(both, [(1, 2), (2, 1), (2, -1), (-1, 0), (-1, 1)]))
    swap([(2, 2)], t, e4)
    first = products([mine], [(2, 2)])
    swap([(-1, -1)], first, t)
    swap([(-1, 2)], first, t)
    products([mine], [(-1, -1), (-1, 2)])
    products([theirs], [(2, 2)])
    products([theirs], [(-1, -1), (-1, 2)])
    return state["outs"]


def any_rounds(moves, run, lefts, ritz):
    chips, cols = moves.chips, moves.cols
    final = cols + chips - 3
    distances = [*range(cols - 1), -1]
    mine, theirs = {(0, 0): (ritz, 0)}, {}

    def bundle(keys, gate):
        values = [lax.slice_in_dim(a, 2 * n, 2 * n + 2) if a.shape[0] > 2 else a for a, n in (mine[key] for key in keys)]
        if gate:
            values = [after(v, *gate) for v in values]
        return jnp.concatenate(values, 0) if len(values) > 1 else values[0]

    def move(how, into, sources, keys, gate, name):
        if not keys:
            return ()
        with jax.named_scope(name):
            value = how(bundle(sources, gate))
        into.update({key: (value, number) for number, key in enumerate(keys)})
        return (value,)

    def part(layer, hops, begun=None, finish=True):
        return Part(layer, [(h, whose is mine, *whose[layer, h]) for whose in (mine, theirs) for h in hops], () if begun is None else (begun,), finish)

    def complete(layer):
        return [*range(chips - 1), -1] if layer in (0, -1) else [*range(chips)]

    state = {"outs": None}
    sums, used = {}, {d: [] for d in distances}

    def products(keys):
        parts = []
        for d in distances:
            hops = [h for h in complete(d) if (d, h) in keys and h not in used[d]]
            if hops:
                used[d] += hops
                parts.append(part(d, hops, sums.pop(d, None), len(used[d]) == len(complete(d))))
        parts.sort(key=lambda p: p.finish)
        state["outs"], kept = run(parts, outs=state["outs"])
        unfinished = [p for p in parts if not p.finish]
        sums.update({p.stage: s for p, s in zip(unfinished, kept, strict=True)})
        return kept[0] if unfinished else state["outs"][0]

    def tiny(value, number):
        at = 16 * (number % (ritz.shape[1] // 16))
        with jax.named_scope("token"):
            return moves.other(after(lax.slice(ritz, (0, at, 0), (1, at + 16, 128)), value))

    along_gate = gate = ()
    fresh = [(0, 0)]
    for r in range(1, final + 1):
        if r < cols - 1:
            layer, hop, step = r, 0, 1
        else:
            layer, hop, step = -1, r - (cols - 1), -1
        source = (layer - step, hop)
        z = move(lambda v: moves.along(v, step), mine, [source], [(layer, hop)], along_gate, f"along{layer}_{hop}")
        ring = [(d, r - d) for d in range(cols - 1) if 1 <= r - d <= (chips - 2 if d == 0 else chips - 1)]
        p = move(lambda v: moves.ring(v, 1), mine, [(d, h - 1) for d, h in ring], ring, gate, f"ring{r}")
        back = {1: [(0, -1)], final: [(-1, -1)]}.get(r, [])
        m = move(lambda v: moves.ring(v, -1), mine, [(d, 0) for d, _ in back], back, gate, f"back{r}")
        e = move(moves.other, theirs, fresh, fresh, gate, f"core{r}")
        fresh_before, fresh = fresh, [*ring, (layer, hop), *back]
        token = ()
        held = set(theirs) - set(fresh_before)
        if r >= chips:
            ran = products(held)
            if r == final:
                ran = products(set(theirs))
            token = (tiny(ran, r),)
        along_gate = (*p, *m, *e, *token, *(lefts if r == 1 else ()))
        gate = (*along_gate, *z)
    for key in [key for key in fresh if key != (layer, hop)]:
        move(moves.other, theirs, [key], [key], token, f"core_last{key[0]}_{key[1]}")
    products(set(theirs))
    move(moves.other, theirs, [(layer, hop)], [(layer, hop)], (), "core_end")
    products(set(theirs))
    return state["outs"]


def shards(rows, cols, orbitals, applied, ritz):
    moves = Moves(rows, cols)
    lefts = [x.reshape(x.shape[0], -1) for x in (orbitals, applied)]
    run = functools.partial(run_parts, rows=rows, cols=cols, lefts=lefts, like=orbitals)
    return (few_rounds if (moves.chips, cols) == (4, 4) else any_rounds)(moves, run, lefts, ritz)


def solution(mesh):
    rows, cols = mesh.shape["row"], mesh.shape["col"]
    whole = P(AXES, None, None)
    return jax.shard_map(
        functools.partial(shards, rows, cols),
        mesh=mesh,
        in_specs=(whole, whole, P(None, "row", "col")),
        out_specs=(whole, whole),
        check_vma=False,
    )
```

```python
import functools

import jax
import jax.numpy as jnp
from jax import lax
from jax.experimental import pallas as pl
from jax.experimental.pallas import tpu as pltpu
from jax.sharding import PartitionSpec as P

AXES = ("row", "col")


def chip_at(place, chips):
    place = place % chips
    return 2 * place if 2 * place < chips else 2 * (chips - 1 - place) + 1


class Moves:
    def __init__(self, rows, cols):
        self.chips, self.cols = rows // 2, cols

    def every(self):
        for place in range(self.chips):
            for core in range(2):
                for layer in range(self.cols):
                    yield place, core, layer

    def device(self, place, core, layer):
        return (chip_at(place, self.chips) * 2 + core) * self.cols + layer % self.cols

    def ring(self, value, step):
        pairs = [(self.device(p, k, z), self.device(p + (step if k == 0 else -step), k, z)) for p, k, z in self.every()]
        return lax.ppermute(value, AXES, pairs)

    def along(self, value, step):
        pairs = [(self.device(p, k, z), self.device(p, k, z + step)) for p, k, z in self.every()]
        return lax.ppermute(value, AXES, pairs)

    def other(self, value):
        pairs = [(self.device(p, k, z), self.device(p, 1 - k, z)) for p, k, z in self.every()]
        return lax.ppermute(value, AXES, pairs)


def after(value, *earlier):
    return lax.optimization_barrier((value,) + earlier)[0]


class Part:
    def __init__(self, stage, terms, begun=(), finish=True):
        self.stage, self.terms, self.begun, self.finish = stage, terms, begun, finish


def parts_kernel(plan, rows, cols, n_arrays, n_outs, fresh, first, second, *refs):
    refs = list(refs)
    arrays = [refs.pop(0) for _ in range(n_arrays)]
    begun = [[refs.pop(0) for _ in range(count)] for _, _, count, _ in plan]
    if n_outs and not fresh:
        del refs[:2]
    outs = [refs.pop(0) for _ in range(n_outs)]
    sums = [None if finish else refs.pop(0) for _, _, _, finish in plan]
    chips = rows // 2
    depth, width = arrays[0].shape[1:]
    g, bands = first.shape[0], first.shape[1] // 2
    row, layer = lax.axis_index("row"), lax.axis_index("col")
    chip, core = row // 2, row % 2
    place = jnp.where(chip % 2 == 0, chip // 2, chips - 1 - chip // 2)
    copies = []
    for i, (stage, terms, _, finish) in enumerate(plan):
        total = jnp.zeros((4 * g, width), jnp.float32) if not begun[i] else functools.reduce(jnp.add, [b[...] for b in begun[i]])
        for hop, mine, array, number in terms:
            owner_core = core if mine else 1 - core
            at = (place + chips + jnp.where(owner_core == 0, -hop, hop)) % chips
            owner = jnp.where(2 * at < chips, 2 * at, 2 * (chips - 1 - at) + 1) * 2 + owner_core
            real = pl.ds(pl.multiple_of(owner * depth, depth), depth)
            imag = pl.ds(pl.multiple_of(bands + owner * depth, depth), depth)
            left = [jnp.concatenate([x[:, real], -x[:, imag]], 1) for x in (first, second)]
            left += [jnp.concatenate([x[:, imag], x[:, real]], 1) for x in (first, second)]
            right = arrays[array][2 * number : 2 * number + 2].reshape(2 * depth, width)
            total += jnp.dot(jnp.concatenate(left, 0), right, preferred_element_type=jnp.float32)
        if not finish:
            sums[i][...] = total
            continue
        rounded = total.astype(outs[0].dtype)
        columns = pl.ds(pl.multiple_of(((layer + cols - stage) % cols) * width, width), width)
        for half in range(2):
            tile, sem = refs.pop(0), refs.pop(0)
            tile[:, 0, :] = rounded[half * g : (half + 1) * g]
            tile[:, 1, :] = rounded[(2 + half) * g : (3 + half) * g]
            copy = pltpu.make_async_copy(tile, outs[half].at[:, :, columns], sem)
            copy.start()
            copies.append(copy)
    for copy in copies:
        copy.wait()


def run_parts(parts, rows, cols, lefts, like, outs=None, weight=1):
    g = like.shape[0]
    fresh = outs is None
    finishing = sum(p.finish for p in parts)
    vmem, hbm = pl.BlockSpec(memory_space=pltpu.VMEM), pl.BlockSpec(memory_space=pl.ANY)
    arrays = list({id(t[2]): t[2] for p in parts for t in p.terms}.values())
    index = {id(a): i for i, a in enumerate(arrays)}
    depth, width = arrays[0].shape[1:]
    operands = [*lefts, *arrays, *(b for p in parts for b in p.begun)]
    in_specs = [vmem] * len(operands)
    out_shape, out_specs, scratch, aliases = [], [], [], {}
    if finishing:
        if not fresh:
            aliases = {len(operands): 0, len(operands) + 1: 1}
            operands, in_specs = [*operands, *outs], [*in_specs, hbm, hbm]
        out_shape, out_specs = [jax.ShapeDtypeStruct(like.shape, like.dtype)] * 2, [hbm, hbm]
        scratch = [pltpu.VMEM((g, 2, width), like.dtype), pltpu.SemaphoreType.DMA] * 2 * finishing
    sums = len(parts) - finishing
    out_shape += [jax.ShapeDtypeStruct((4 * g, width), jnp.float32)] * sums
    out_specs += [vmem] * sums
    count = sum(len(p.terms) for p in parts)
    plan = [(p.stage, [(h, m, index[id(a)], n) for h, m, a, n in p.terms], len(p.begun), p.finish) for p in parts]
    result = pl.pallas_call(
        functools.partial(parts_kernel, plan, rows, cols, len(arrays), 2 if finishing else 0, fresh),
        out_shape=out_shape,
        in_specs=in_specs,
        out_specs=out_specs,
        scratch_shapes=scratch,
        input_output_aliases=aliases,
        compiler_params=pltpu.CompilerParams(vmem_limit_bytes=28 * 2**20),
        cost_estimate=pl.CostEstimate(flops=weight * 2 * 8 * g * depth * width * count, bytes_accessed=max(1, min(weight, 1) * 2**20 * count), transcendentals=0),
    )(*operands)
    return (tuple(result[:2]), result[2:]) if finishing else (outs, result)


def few_rounds(moves, run, lefts, ritz):
    distances = [0, 1, 2, -1]
    mine, theirs = {(0, 0): (ritz, 0)}, {}
    full = {0: [0, 1, 2, -1], 1: [0, 1, 2, -1], 2: [0, 1, 2, -1], -1: [0, 1, 2, -1]}

    def bundle(keys, gate):
        values = [lax.slice_in_dim(a, 2 * n, 2 * n + 2) if a.shape[0] > 2 else a for a, n in (mine[key] for key in keys)]
        values = [after(v, *gate) for v in values]
        return jnp.concatenate(values, 0) if len(values) > 1 else values[0]

    def move(how, step, pairs, *gate):
        with jax.named_scope(how + "_".join(f"{d}:{h}" for _, (d, h) in pairs)):
            value = getattr(moves, how)(bundle([source for source, _ in pairs], gate), step)
        mine.update({key: (value, number) for number, (_, key) in enumerate(pairs)})
        return value

    def swap(keys, *gate):
        with jax.named_scope("core" + "_".join(f"{d}:{h}" for d, h in keys)):
            value = moves.other(bundle(keys, gate))
        theirs.update({key: (value, number) for number, key in enumerate(keys)})
        return value

    state = {"outs": None, "tokens": 0}
    sums, used = {d: [] for d in distances}, {d: [] for d in distances}

    def products(who, keys, fresh=(), more=(), weight=1):
        parts = []
        for d in distances:
            terms = [(h, whose is mine, *whose[d, h]) for whose in who for e, h in keys if e == d]
            terms += [(h, whose is mine, *whose[d, h]) for whose, e, h in more if e == d]
            if terms:
                used[d] += terms
                begun = []
                if d not in fresh:
                    begun, sums[d] = sums[d], []
                parts.append(Part(d, terms, begun, d not in fresh and len(used[d]) == 2 * len(full[d])))
        parts.sort(key=lambda p: p.finish)
        state["outs"], kept = run(parts, outs=state["outs"], weight=weight)
        unfinished = [p for p in parts if not p.finish]
        for p, s in zip(unfinished, kept, strict=True):
            sums[p.stage].append(s)
        return kept[0] if unfinished else state["outs"][0]

    def token(value):
        at = 16 * state["tokens"]
        state["tokens"] += 1
        with jax.named_scope("token"):
            return moves.other(after(lax.slice(ritz, (0, at, 0), (1, at + 16, 128)), value))

    both = (mine, theirs)
    cut = ritz.shape[1] // 2

    def down(value, name, *gate):
        with jax.named_scope(name):
            return moves.along(after(value, *gate), -1)

    z1 = move("along", 1, [((0, 0), (1, 0))])
    p1 = move("ring", 1, [((0, 0), (0, 1))])
    m1 = move("ring", -1, [((0, 0), (0, -1))], p1, *lefts)
    e1 = swap([(0, 0)], p1, *lefts)
    x2 = move("ring", 1, [((0, 1), (0, 2))], *lefts)
    gate = (p1, z1)
    z2 = move("along", 1, [((1, 0), (2, 0))], *gate)
    s1 = move("ring", 1, [((1, 0), (1, 1))], *gate)
    m2 = move("ring", -1, [((1, 0), (1, -1))], m1, *gate)
    upper = down(ritz[:, :cut], "along_upper", m1, *gate)
    gate = (lax.slice(x2, (0, 0, 0), (1, 16, 128)), s1, m2, e1, z2, upper)
    p3 = move("ring", 1, [((1, 1), (1, 2)), ((2, 0), (2, 1))], *gate)
    lower = down(jnp.concatenate([ritz[:, cut:], mine[0, 1][0]], 1), "along_lower", *gate)
    e3 = swap([(0, 1), (0, -1), (0, 2), (1, 0)], *gate)
    e3b = swap([(1, 1), (1, -1), (2, 0)], *gate)
    m3 = move("ring", -1, [((2, 0), (2, -1))], e3, *gate)
    products(both, [(0, 0), (0, 1), (0, -1), (0, 2), (1, 0)], weight=0)
    t = token(products(both, [(1, 1), (1, -1), (2, 0)], weight=0))
    mine[-1, 0] = jnp.concatenate([upper, lower[:, : ritz.shape[1] - cut]], 1), 0
    mine[-1, 1] = lower[:, ritz.shape[1] - cut :], 0
    gate = (p3, m3, e3, t)
    z5 = move("along", -1, [((0, 2), (-1, 2))], m3, e3, t)
    gate = (*gate, lower)
    p4 = move("ring", 1, [((2, 1), (2, 2))], *gate)
    e4 = swap([(1, 2), (2, 1), (2, -1)], *gate)
    e4b = swap([(-1, 0), (-1, 1)], *gate)
    m4 = move("ring", -1, [((-1, 0), (-1, -1))], e4b, *gate)
    t = token(products(both, [(1, 2), (2, 1), (2, -1), (-1, 0), (-1, 1)]))
    swap([(2, 2)], t, e4)
    first = products([mine], [(2, 2)])
    swap([(-1, -1)], first, t)
    swap([(-1, 2)], first, t)
    products([mine], [(-1, -1), (-1, 2)])
    products([theirs], [(2, 2)])
    products([theirs], [(-1, -1), (-1, 2)])
    return state["outs"]


def any_rounds(moves, run, lefts, ritz):
    chips, cols = moves.chips, moves.cols
    final = cols + chips - 3
    distances = [*range(cols - 1), -1]
    mine, theirs = {(0, 0): (ritz, 0)}, {}

    def bundle(keys, gate):
        values = [lax.slice_in_dim(a, 2 * n, 2 * n + 2) if a.shape[0] > 2 else a for a, n in (mine[key] for key in keys)]
        if gate:
            values = [after(v, *gate) for v in values]
        return jnp.concatenate(values, 0) if len(values) > 1 else values[0]

    def move(how, into, sources, keys, gate, name):
        if not keys:
            return ()
        with jax.named_scope(name):
            value = how(bundle(sources, gate))
        into.update({key: (value, number) for number, key in enumerate(keys)})
        return (value,)

    def part(layer, hops, begun=None, finish=True):
        return Part(layer, [(h, whose is mine, *whose[layer, h]) for whose in (mine, theirs) for h in hops], () if begun is None else (begun,), finish)

    def complete(layer):
        return [*range(chips - 1), -1] if layer in (0, -1) else [*range(chips)]

    state = {"outs": None}
    sums, used = {}, {d: [] for d in distances}

    def products(keys):
        parts = []
        for d in distances:
            hops = [h for h in complete(d) if (d, h) in keys and h not in used[d]]
            if hops:
                used[d] += hops
                parts.append(part(d, hops, sums.pop(d, None), len(used[d]) == len(complete(d))))
        parts.sort(key=lambda p: p.finish)
        state["outs"], kept = run(parts, outs=state["outs"])
        unfinished = [p for p in parts if not p.finish]
        sums.update({p.stage: s for p, s in zip(unfinished, kept, strict=True)})
        return kept[0] if unfinished else state["outs"][0]

    def tiny(value, number):
        at = 16 * (number % (ritz.shape[1] // 16))
        with jax.named_scope("token"):
            return moves.other(after(lax.slice(ritz, (0, at, 0), (1, at + 16, 128)), value))

    along_gate = gate = ()
    fresh = [(0, 0)]
    for r in range(1, final + 1):
        if r < cols - 1:
            layer, hop, step = r, 0, 1
        else:
            layer, hop, step = -1, r - (cols - 1), -1
        source = (layer - step, hop)
        z = move(lambda v: moves.along(v, step), mine, [source], [(layer, hop)], along_gate, f"along{layer}_{hop}")
        ring = [(d, r - d) for d in range(cols - 1) if 1 <= r - d <= (chips - 2 if d == 0 else chips - 1)]
        p = move(lambda v: moves.ring(v, 1), mine, [(d, h - 1) for d, h in ring], ring, gate, f"ring{r}")
        back = {1: [(0, -1)], final: [(-1, -1)]}.get(r, [])
        m = move(lambda v: moves.ring(v, -1), mine, [(d, 0) for d, _ in back], back, gate, f"back{r}")
        e = move(moves.other, theirs, fresh, fresh, gate, f"core{r}")
        fresh_before, fresh = fresh, [*ring, (layer, hop), *back]
        token = ()
        held = set(theirs) - set(fresh_before)
        if r >= chips:
            ran = products(held)
            if r == final:
                ran = products(set(theirs))
            token = (tiny(ran, r),)
        along_gate = (*p, *m, *e, *token, *(lefts if r == 1 else ()))
        gate = (*along_gate, *z)
    for key in [key for key in fresh if key != (layer, hop)]:
        move(moves.other, theirs, [key], [key], token, f"core_last{key[0]}_{key[1]}")
    products(set(theirs))
    move(moves.other, theirs, [(layer, hop)], [(layer, hop)], (), "core_end")
    products(set(theirs))
    return state["outs"]


def shards(rows, cols, orbitals, applied, ritz):
    moves = Moves(rows, cols)
    lefts = [x.reshape(x.shape[0], -1) for x in (orbitals, applied)]
    run = functools.partial(run_parts, rows=rows, cols=cols, lefts=lefts, like=orbitals)
    return (few_rounds if (moves.chips, cols) == (4, 4) else any_rounds)(moves, run, lefts, ritz)


def solution(mesh):
    rows, cols = mesh.shape["row"], mesh.shape["col"]
    whole = P(AXES, None, None)
    return jax.shard_map(
        functools.partial(shards, rows, cols),
        mesh=mesh,
        in_specs=(whole, whole, P(None, "row", "col")),
        out_specs=(whole, whole),
        check_vma=False,
    )
```

```python
import functools

import jax
import jax.numpy as jnp
from jax import lax
from jax.experimental import pallas as pl
from jax.experimental.pallas import tpu as pltpu
from jax.sharding import PartitionSpec as P

AXES = ("row", "col")


def chip_at(place, chips):
    place = place % chips
    return 2 * place if 2 * place < chips else 2 * (chips - 1 - place) + 1


class Moves:
    def __init__(self, rows, cols):
        self.chips, self.cols = rows // 2, cols

    def every(self):
        for place in range(self.chips):
            for core in range(2):
                for layer in range(self.cols):
                    yield place, core, layer

    def device(self, place, core, layer):
        return (chip_at(place, self.chips) * 2 + core) * self.cols + layer % self.cols

    def ring(self, value, step):
        pairs = [(self.device(p, k, z), self.device(p + (step if k == 0 else -step), k, z)) for p, k, z in self.every()]
        return lax.ppermute(value, AXES, pairs)

    def along(self, value, step):
        pairs = [(self.device(p, k, z), self.device(p, k, z + step)) for p, k, z in self.every()]
        return lax.ppermute(value, AXES, pairs)

    def other(self, value):
        pairs = [(self.device(p, k, z), self.device(p, 1 - k, z)) for p, k, z in self.every()]
        return lax.ppermute(value, AXES, pairs)


def after(value, *earlier):
    return lax.optimization_barrier((value,) + earlier)[0]


class Part:
    def __init__(self, stage, terms, begun=(), finish=True):
        self.stage, self.terms, self.begun, self.finish = stage, terms, begun, finish


def parts_kernel(plan, rows, cols, n_arrays, n_outs, fresh, first, second, *refs):
    refs = list(refs)
    arrays = [refs.pop(0) for _ in range(n_arrays)]
    begun = [[refs.pop(0) for _ in range(count)] for _, _, count, _ in plan]
    if n_outs and not fresh:
        del refs[:2]
    outs = [refs.pop(0) for _ in range(n_outs)]
    sums = [None if finish else refs.pop(0) for _, _, _, finish in plan]
    chips = rows // 2
    depth, width = arrays[0].shape[1:]
    g, bands = first.shape[0], first.shape[1] // 2
    row, layer = lax.axis_index("row"), lax.axis_index("col")
    chip, core = row // 2, row % 2
    place = jnp.where(chip % 2 == 0, chip // 2, chips - 1 - chip // 2)
    copies = []
    for i, (stage, terms, _, finish) in enumerate(plan):
        total = jnp.zeros((4 * g, width), jnp.float32) if not begun[i] else functools.reduce(jnp.add, [b[...] for b in begun[i]])
        for hop, mine, array, number in terms:
            owner_core = core if mine else 1 - core
            at = (place + chips + jnp.where(owner_core == 0, -hop, hop)) % chips
            owner = jnp.where(2 * at < chips, 2 * at, 2 * (chips - 1 - at) + 1) * 2 + owner_core
            real = pl.ds(pl.multiple_of(owner * depth, depth), depth)
            imag = pl.ds(pl.multiple_of(bands + owner * depth, depth), depth)
            left = [jnp.concatenate([x[:, real], -x[:, imag]], 1) for x in (first, second)]
            left += [jnp.concatenate([x[:, imag], x[:, real]], 1) for x in (first, second)]
            right = arrays[array][2 * number : 2 * number + 2].reshape(2 * depth, width)
            total += jnp.dot(jnp.concatenate(left, 0), right, preferred_element_type=jnp.float32)
        if not finish:
            sums[i][...] = total
            continue
        rounded = total.astype(outs[0].dtype)
        columns = pl.ds(pl.multiple_of(((layer + cols - stage) % cols) * width, width), width)
        for half in range(2):
            tile, sem = refs.pop(0), refs.pop(0)
            tile[:, 0, :] = rounded[half * g : (half + 1) * g]
            tile[:, 1, :] = rounded[(2 + half) * g : (3 + half) * g]
            copy = pltpu.make_async_copy(tile, outs[half].at[:, :, columns], sem)
            copy.start()
            copies.append(copy)
    for copy in copies:
        copy.wait()


def run_parts(parts, rows, cols, lefts, like, outs=None, weight=1):
    g = like.shape[0]
    fresh = outs is None
    finishing = sum(p.finish for p in parts)
    vmem, hbm = pl.BlockSpec(memory_space=pltpu.VMEM), pl.BlockSpec(memory_space=pl.ANY)
    arrays = list({id(t[2]): t[2] for p in parts for t in p.terms}.values())
    index = {id(a): i for i, a in enumerate(arrays)}
    depth, width = arrays[0].shape[1:]
    operands = [*lefts, *arrays, *(b for p in parts for b in p.begun)]
    in_specs = [vmem] * len(operands)
    out_shape, out_specs, scratch, aliases = [], [], [], {}
    if finishing:
        if not fresh:
            aliases = {len(operands): 0, len(operands) + 1: 1}
            operands, in_specs = [*operands, *outs], [*in_specs, hbm, hbm]
        out_shape, out_specs = [jax.ShapeDtypeStruct(like.shape, like.dtype)] * 2, [hbm, hbm]
        scratch = [pltpu.VMEM((g, 2, width), like.dtype), pltpu.SemaphoreType.DMA] * 2 * finishing
    sums = len(parts) - finishing
    out_shape += [jax.ShapeDtypeStruct((4 * g, width), jnp.float32)] * sums
    out_specs += [vmem] * sums
    count = sum(len(p.terms) for p in parts)
    plan = [(p.stage, [(h, m, index[id(a)], n) for h, m, a, n in p.terms], len(p.begun), p.finish) for p in parts]
    result = pl.pallas_call(
        functools.partial(parts_kernel, plan, rows, cols, len(arrays), 2 if finishing else 0, fresh),
        out_shape=out_shape,
        in_specs=in_specs,
        out_specs=out_specs,
        scratch_shapes=scratch,
        input_output_aliases=aliases,
        compiler_params=pltpu.CompilerParams(vmem_limit_bytes=28 * 2**20),
        cost_estimate=pl.CostEstimate(flops=weight * 2 * 8 * g * depth * width * count, bytes_accessed=max(1, min(weight, 1) * 2**20 * count), transcendentals=0),
    )(*operands)
    return (tuple(result[:2]), result[2:]) if finishing else (outs, result)


def few_rounds(moves, run, lefts, ritz):
    distances = [0, 1, 2, -1]
    mine, theirs = {(0, 0): (ritz, 0)}, {}
    full = {0: [0, 1, 2, -1], 1: [0, 1, 2, -1], 2: [0, 1, 2, -1], -1: [0, 1, 2, -1]}

    def bundle(keys, gate):
        values = [lax.slice_in_dim(a, 2 * n, 2 * n + 2) if a.shape[0] > 2 else a for a, n in (mine[key] for key in keys)]
        values = [after(v, *gate) for v in values]
        return jnp.concatenate(values, 0) if len(values) > 1 else values[0]

    def move(how, step, pairs, *gate):
        with jax.named_scope(how + "_".join(f"{d}:{h}" for _, (d, h) in pairs)):
            value = getattr(moves, how)(bundle([source for source, _ in pairs], gate), step)
        mine.update({key: (value, number) for number, (_, key) in enumerate(pairs)})
        return value

    def swap(keys, *gate):
        with jax.named_scope("core" + "_".join(f"{d}:{h}" for d, h in keys)):
            value = moves.other(bundle(keys, gate))
        theirs.update({key: (value, number) for number, key in enumerate(keys)})
        return value

    state = {"outs": None, "tokens": 0}
    sums, used = {d: [] for d in distances}, {d: [] for d in distances}

    def products(who, keys, fresh=(), more=(), weight=1):
        parts = []
        for d in distances:
            terms = [(h, whose is mine, *whose[d, h]) for whose in who for e, h in keys if e == d]
            terms += [(h, whose is mine, *whose[d, h]) for whose, e, h in more if e == d]
            if terms:
                used[d] += terms
                begun = []
                if d not in fresh:
                    begun, sums[d] = sums[d], []
                parts.append(Part(d, terms, begun, d not in fresh and len(used[d]) == 2 * len(full[d])))
        parts.sort(key=lambda p: p.finish)
        state["outs"], kept = run(parts, outs=state["outs"], weight=weight)
        unfinished = [p for p in parts if not p.finish]
        for p, s in zip(unfinished, kept, strict=True):
            sums[p.stage].append(s)
        return kept[0] if unfinished else state["outs"][0]

    def token(value):
        at = 16 * state["tokens"]
        state["tokens"] += 1
        with jax.named_scope("token"):
            return moves.other(after(lax.slice(ritz, (0, at, 0), (1, at + 16, 128)), value))

    both = (mine, theirs)
    cut = ritz.shape[1] // 2

    def down(value, name, *gate):
        with jax.named_scope(name):
            return moves.along(after(value, *gate), -1)

    z1 = move("along", 1, [((0, 0), (1, 0))])
    p1 = move("ring", 1, [((0, 0), (0, 1))])
    m1 = move("ring", -1, [((0, 0), (0, -1))], *lefts)
    e1 = swap([(0, 0)], p1, *lefts)
    x2 = move("ring", 1, [((0, 1), (0, 2))])
    gate = (p1, z1)
    z2 = move("along", 1, [((1, 0), (2, 0))], *gate)
    s1 = move("ring", 1, [((1, 0), (1, 1))], *gate)
    m2 = move("ring", -1, [((1, 0), (1, -1))], m1, *gate)
    upper = down(ritz[:, :cut], "along_upper", m1, *gate)
    gate = (lax.slice(x2, (0, 0, 0), (1, 16, 128)), s1, m2, e1, z2, upper)
    p3 = move("ring", 1, [((1, 1), (1, 2)), ((2, 0), (2, 1))], *gate)
    lower = down(jnp.concatenate([ritz[:, cut:], mine[0, 1][0]], 1), "along_lower", *gate)
    e3 = swap([(0, 1), (0, -1), (0, 2), (1, 0)], *gate)
    e3b = swap([(1, 1), (1, -1), (2, 0)], *gate)
    m3 = move("ring", -1, [((2, 0), (2, -1))], e3, *gate)
    products(both, [(0, 0), (0, 1), (0, -1), (0, 2), (1, 0)], weight=0)
    t = token(products(both, [(1, 1), (1, -1), (2, 0)], weight=0))
    mine[-1, 0] = jnp.concatenate([upper, lower[:, : ritz.shape[1] - cut]], 1), 0
    mine[-1, 1] = lower[:, ritz.shape[1] - cut :], 0
    gate = (p3, m3, e3, t)
    z5 = move("along", -1, [((0, 2), (-1, 2))], m3, e3, t)
    gate = (*gate, lower)
    p4 = move("ring", 1, [((2, 1), (2, 2))], *gate)
    e4 = swap([(1, 2), (2, 1), (2, -1)], *gate)
    e4b = swap([(-1, 0), (-1, 1)], *gate)
    m4 = move("ring", -1, [((-1, 0), (-1, -1))], e4b, *gate)
    t = products(both, [(1, 2), (2, 1), (2, -1), (-1, 0), (-1, 1)])
    swap([(2, 2)], t, e4)
    first = products([mine], [(2, 2)])
    swap([(-1, -1)], first, t)
    swap([(-1, 2)], first, t)
    products([mine], [(-1, -1), (-1, 2)])
    products([theirs], [(2, 2)])
    products([theirs], [(-1, -1), (-1, 2)])
    return state["outs"]


def any_rounds(moves, run, lefts, ritz):
    chips, cols = moves.chips, moves.cols
    final = cols + chips - 3
    distances = [*range(cols - 1), -1]
    mine, theirs = {(0, 0): (ritz, 0)}, {}

    def bundle(keys, gate):
        values = [lax.slice_in_dim(a, 2 * n, 2 * n + 2) if a.shape[0] > 2 else a for a, n in (mine[key] for key in keys)]
        if gate:
            values = [after(v, *gate) for v in values]
        return jnp.concatenate(values, 0) if len(values) > 1 else values[0]

    def move(how, into, sources, keys, gate, name):
        if not keys:
            return ()
        with jax.named_scope(name):
            value = how(bundle(sources, gate))
        into.update({key: (value, number) for number, key in enumerate(keys)})
        return (value,)

    def part(layer, hops, begun=None, finish=True):
        return Part(layer, [(h, whose is mine, *whose[layer, h]) for whose in (mine, theirs) for h in hops], () if begun is None else (begun,), finish)

    def complete(layer):
        return [*range(chips - 1), -1] if layer in (0, -1) else [*range(chips)]

    state = {"outs": None}
    sums, used = {}, {d: [] for d in distances}

    def products(keys):
        parts = []
        for d in distances:
            hops = [h for h in complete(d) if (d, h) in keys and h not in used[d]]
            if hops:
                used[d] += hops
                parts.append(part(d, hops, sums.pop(d, None), len(used[d]) == len(complete(d))))
        parts.sort(key=lambda p: p.finish)
        state["outs"], kept = run(parts, outs=state["outs"])
        unfinished = [p for p in parts if not p.finish]
        sums.update({p.stage: s for p, s in zip(unfinished, kept, strict=True)})
        return kept[0] if unfinished else state["outs"][0]

    def tiny(value, number):
        at = 16 * (number % (ritz.shape[1] // 16))
        with jax.named_scope("token"):
            return moves.other(after(lax.slice(ritz, (0, at, 0), (1, at + 16, 128)), value))

    along_gate = gate = ()
    fresh = [(0, 0)]
    for r in range(1, final + 1):
        if r < cols - 1:
            layer, hop, step = r, 0, 1
        else:
            layer, hop, step = -1, r - (cols - 1), -1
        source = (layer - step, hop)
        z = move(lambda v: moves.along(v, step), mine, [source], [(layer, hop)], along_gate, f"along{layer}_{hop}")
        ring = [(d, r - d) for d in range(cols - 1) if 1 <= r - d <= (chips - 2 if d == 0 else chips - 1)]
        p = move(lambda v: moves.ring(v, 1), mine, [(d, h - 1) for d, h in ring], ring, gate, f"ring{r}")
        back = {1: [(0, -1)], final: [(-1, -1)]}.get(r, [])
        m = move(lambda v: moves.ring(v, -1), mine, [(d, 0) for d, _ in back], back, gate, f"back{r}")
        e = move(moves.other, theirs, fresh, fresh, gate, f"core{r}")
        fresh_before, fresh = fresh, [*ring, (layer, hop), *back]
        token = ()
        held = set(theirs) - set(fresh_before)
        if r >= chips:
            ran = products(held)
            if r == final:
                ran = products(set(theirs))
            token = (tiny(ran, r),)
        along_gate = (*p, *m, *e, *token, *(lefts if r == 1 else ()))
        gate = (*along_gate, *z)
    for key in [key for key in fresh if key != (layer, hop)]:
        move(moves.other, theirs, [key], [key], token, f"core_last{key[0]}_{key[1]}")
    products(set(theirs))
    move(moves.other, theirs, [(layer, hop)], [(layer, hop)], (), "core_end")
    products(set(theirs))
    return state["outs"]


def shards(rows, cols, orbitals, applied, ritz):
    moves = Moves(rows, cols)
    lefts = [x.reshape(x.shape[0], -1) for x in (orbitals, applied)]
    run = functools.partial(run_parts, rows=rows, cols=cols, lefts=lefts, like=orbitals)
    return (few_rounds if (moves.chips, cols) == (4, 4) else any_rounds)(moves, run, lefts, ritz)


def solution(mesh):
    rows, cols = mesh.shape["row"], mesh.shape["col"]
    whole = P(AXES, None, None)
    return jax.shard_map(
        functools.partial(shards, rows, cols),
        mesh=mesh,
        in_specs=(whole, whole, P(None, "row", "col")),
        out_specs=(whole, whole),
        check_vma=False,
    )
```

```python
import functools

import jax
import jax.numpy as jnp
from jax import lax
from jax.experimental import pallas as pl
from jax.experimental.pallas import tpu as pltpu
from jax.sharding import PartitionSpec as P

AXES = ("row", "col")


def chip_at(place, chips):
    place = place % chips
    return 2 * place if 2 * place < chips else 2 * (chips - 1 - place) + 1


class Moves:
    def __init__(self, rows, cols):
        self.chips, self.cols = rows // 2, cols

    def every(self):
        for place in range(self.chips):
            for core in range(2):
                for layer in range(self.cols):
                    yield place, core, layer

    def device(self, place, core, layer):
        return (chip_at(place, self.chips) * 2 + core) * self.cols + layer % self.cols

    def ring(self, value, step):
        pairs = [(self.device(p, k, z), self.device(p + (step if k == 0 else -step), k, z)) for p, k, z in self.every()]
        return lax.ppermute(value, AXES, pairs)

    def along(self, value, step):
        pairs = [(self.device(p, k, z), self.device(p, k, z + step)) for p, k, z in self.every()]
        return lax.ppermute(value, AXES, pairs)

    def other(self, value):
        pairs = [(self.device(p, k, z), self.device(p, 1 - k, z)) for p, k, z in self.every()]
        return lax.ppermute(value, AXES, pairs)


def after(value, *earlier):
    return lax.optimization_barrier((value,) + earlier)[0]


class Part:
    def __init__(self, stage, terms, begun=(), finish=True):
        self.stage, self.terms, self.begun, self.finish = stage, terms, begun, finish


def parts_kernel(plan, rows, cols, n_arrays, n_outs, fresh, first, second, *refs):
    refs = list(refs)
    arrays = [refs.pop(0) for _ in range(n_arrays)]
    begun = [[refs.pop(0) for _ in range(count)] for _, _, count, _ in plan]
    if n_outs and not fresh:
        del refs[:2]
    outs = [refs.pop(0) for _ in range(n_outs)]
    sums = [None if finish else refs.pop(0) for _, _, _, finish in plan]
    chips = rows // 2
    depth, width = arrays[0].shape[1:]
    g, bands = first.shape[0], first.shape[1] // 2
    row, layer = lax.axis_index("row"), lax.axis_index("col")
    chip, core = row // 2, row % 2
    place = jnp.where(chip % 2 == 0, chip // 2, chips - 1 - chip // 2)
    copies = []
    for i, (stage, terms, _, finish) in enumerate(plan):
        total = jnp.zeros((4 * g, width), jnp.float32) if not begun[i] else functools.reduce(jnp.add, [b[...] for b in begun[i]])
        for hop, mine, array, number in terms:
            owner_core = core if mine else 1 - core
            at = (place + chips + jnp.where(owner_core == 0, -hop, hop)) % chips
            owner = jnp.where(2 * at < chips, 2 * at, 2 * (chips - 1 - at) + 1) * 2 + owner_core
            real = pl.ds(pl.multiple_of(owner * depth, depth), depth)
            imag = pl.ds(pl.multiple_of(bands + owner * depth, depth), depth)
            left = [jnp.concatenate([x[:, real], -x[:, imag]], 1) for x in (first, second)]
            left += [jnp.concatenate([x[:, imag], x[:, real]], 1) for x in (first, second)]
            right = arrays[array][2 * number : 2 * number + 2].reshape(2 * depth, width)
            total += jnp.dot(jnp.concatenate(left, 0), right, preferred_element_type=jnp.float32)
        if not finish:
            sums[i][...] = total
            continue
        rounded = total.astype(outs[0].dtype)
        columns = pl.ds(pl.multiple_of(((layer + cols - stage) % cols) * width, width), width)
        for half in range(2):
            tile, sem = refs.pop(0), refs.pop(0)
            tile[:, 0, :] = rounded[half * g : (half + 1) * g]
            tile[:, 1, :] = rounded[(2 + half) * g : (3 + half) * g]
            copy = pltpu.make_async_copy(tile, outs[half].at[:, :, columns], sem)
            copy.start()
            copies.append(copy)
    for copy in copies:
        copy.wait()


def run_parts(parts, rows, cols, lefts, like, outs=None, weight=1):
    g = like.shape[0]
    fresh = outs is None
    finishing = sum(p.finish for p in parts)
    vmem, hbm = pl.BlockSpec(memory_space=pltpu.VMEM), pl.BlockSpec(memory_space=pl.ANY)
    arrays = list({id(t[2]): t[2] for p in parts for t in p.terms}.values())
    index = {id(a): i for i, a in enumerate(arrays)}
    depth, width = arrays[0].shape[1:]
    operands = [*lefts, *arrays, *(b for p in parts for b in p.begun)]
    in_specs = [vmem] * len(operands)
    out_shape, out_specs, scratch, aliases = [], [], [], {}
    if finishing:
        if not fresh:
            aliases = {len(operands): 0, len(operands) + 1: 1}
            operands, in_specs = [*operands, *outs], [*in_specs, hbm, hbm]
        out_shape, out_specs = [jax.ShapeDtypeStruct(like.shape, like.dtype)] * 2, [hbm, hbm]
        scratch = [pltpu.VMEM((g, 2, width), like.dtype), pltpu.SemaphoreType.DMA] * 2 * finishing
    sums = len(parts) - finishing
    out_shape += [jax.ShapeDtypeStruct((4 * g, width), jnp.float32)] * sums
    out_specs += [vmem] * sums
    count = sum(len(p.terms) for p in parts)
    plan = [(p.stage, [(h, m, index[id(a)], n) for h, m, a, n in p.terms], len(p.begun), p.finish) for p in parts]
    result = pl.pallas_call(
        functools.partial(parts_kernel, plan, rows, cols, len(arrays), 2 if finishing else 0, fresh),
        out_shape=out_shape,
        in_specs=in_specs,
        out_specs=out_specs,
        scratch_shapes=scratch,
        input_output_aliases=aliases,
        compiler_params=pltpu.CompilerParams(vmem_limit_bytes=28 * 2**20),
        cost_estimate=pl.CostEstimate(flops=weight * 2 * 8 * g * depth * width * count, bytes_accessed=max(1, min(weight, 1) * 2**20 * count), transcendentals=0),
    )(*operands)
    return (tuple(result[:2]), result[2:]) if finishing else (outs, result)


def few_rounds(moves, run, lefts, ritz):
    distances = [0, 1, 2, -1]
    mine, theirs = {(0, 0): (ritz, 0)}, {}
    full = {0: [0, 1, 2, -1], 1: [0, 1, 2, -1], 2: [0, 1, 2, -1], -1: [0, 1, 2, -1]}

    def bundle(keys, gate):
        values = [lax.slice_in_dim(a, 2 * n, 2 * n + 2) if a.shape[0] > 2 else a for a, n in (mine[key] for key in keys)]
        values = [after(v, *gate) for v in values]
        return jnp.concatenate(values, 0) if len(values) > 1 else values[0]

    def move(how, step, pairs, *gate):
        with jax.named_scope(how + "_".join(f"{d}:{h}" for _, (d, h) in pairs)):
            value = getattr(moves, how)(bundle([source for source, _ in pairs], gate), step)
        mine.update({key: (value, number) for number, (_, key) in enumerate(pairs)})
        return value

    def swap(keys, *gate):
        with jax.named_scope("core" + "_".join(f"{d}:{h}" for d, h in keys)):
            value = moves.other(bundle(keys, gate))
        theirs.update({key: (value, number) for number, key in enumerate(keys)})
        return value

    state = {"outs": None, "tokens": 0}
    sums, used = {d: [] for d in distances}, {d: [] for d in distances}

    def products(who, keys, fresh=(), more=(), weight=1):
        parts = []
        for d in distances:
            terms = [(h, whose is mine, *whose[d, h]) for whose in who for e, h in keys if e == d]
            terms += [(h, whose is mine, *whose[d, h]) for whose, e, h in more if e == d]
            if terms:
                used[d] += terms
                begun = []
                if d not in fresh:
                    begun, sums[d] = sums[d], []
                parts.append(Part(d, terms, begun, d not in fresh and len(used[d]) == 2 * len(full[d])))
        parts.sort(key=lambda p: p.finish)
        state["outs"], kept = run(parts, outs=state["outs"], weight=weight)
        unfinished = [p for p in parts if not p.finish]
        for p, s in zip(unfinished, kept, strict=True):
            sums[p.stage].append(s)
        return kept[0] if unfinished else state["outs"][0]

    def token(value):
        at = 16 * state["tokens"]
        state["tokens"] += 1
        with jax.named_scope("token"):
            return moves.other(after(lax.slice(ritz, (0, at, 0), (1, at + 16, 128)), value))

    both = (mine, theirs)
    cut = ritz.shape[1] // 2

    def down(value, name, *gate):
        with jax.named_scope(name):
            return moves.along(after(value, *gate), -1)

    z1 = move("along", 1, [((0, 0), (1, 0))])
    p1 = move("ring", 1, [((0, 0), (0, 1))])
    m1 = move("ring", -1, [((0, 0), (0, -1))], p1, *lefts)
    e1 = swap([(0, 0)], p1, *lefts)
    x2 = move("ring", 1, [((0, 1), (0, 2))], *lefts)
    gate = (p1, z1)
    z2 = move("along", 1, [((1, 0), (2, 0))], *gate)
    s1 = move("ring", 1, [((1, 0), (1, 1))], *gate)
    m2 = move("ring", -1, [((1, 0), (1, -1))], m1, *gate)
    upper = down(ritz[:, :cut], "along_upper", m1, *gate)
    gate = (lax.slice(x2, (0, 0, 0), (1, 16, 128)), s1, m2, e1, z2, upper)
    p3 = move("ring", 1, [((1, 1), (1, 2)), ((2, 0), (2, 1))], *gate)
    lower = down(jnp.concatenate([ritz[:, cut:], mine[0, 1][0]], 1), "along_lower", *gate)
    e3 = swap([(0, 1), (0, -1), (0, 2), (1, 0)], *gate)
    e3b = swap([(1, 1), (1, -1), (2, 0)], *gate)
    m3 = move("ring", -1, [((2, 0), (2, -1))], e3, *gate)
    t = token(products(both, [(0, 0), (0, 1), (0, -1), (0, 2), (1, 0), (1, 1), (1, -1), (2, 0)], weight=0))
    mine[-1, 0] = jnp.concatenate([upper, lower[:, : ritz.shape[1] - cut]], 1), 0
    mine[-1, 1] = lower[:, ritz.shape[1] - cut :], 0
    gate = (p3, m3, e3, t)
    z5 = move("along", -1, [((0, 2), (-1, 2))], m3, e3, t)
    gate = (*gate, lower)
    p4 = move("ring", 1, [((2, 1), (2, 2))], *gate)
    e4 = swap([(1, 2), (2, 1), (2, -1)], *gate)
    e4b = swap([(-1, 0), (-1, 1)], *gate)
    m4 = move("ring", -1, [((-1, 0), (-1, -1))], e4b, *gate)
    t = token(products(both, [(1, 2), (2, 1), (2, -1), (-1, 0), (-1, 1)]))
    swap([(2, 2)], t, e4)
    first = products([mine], [(2, 2)])
    swap([(-1, -1)], first, t)
    swap([(-1, 2)], first, t)
    products([mine], [(-1, -1), (-1, 2)])
    products([theirs], [(2, 2)])
    products([theirs], [(-1, -1), (-1, 2)])
    return state["outs"]


def any_rounds(moves, run, lefts, ritz):
    chips, cols = moves.chips, moves.cols
    final = cols + chips - 3
    distances = [*range(cols - 1), -1]
    mine, theirs = {(0, 0): (ritz, 0)}, {}

    def bundle(keys, gate):
        values = [lax.slice_in_dim(a, 2 * n, 2 * n + 2) if a.shape[0] > 2 else a for a, n in (mine[key] for key in keys)]
        if gate:
            values = [after(v, *gate) for v in values]
        return jnp.concatenate(values, 0) if len(values) > 1 else values[0]

    def move(how, into, sources, keys, gate, name):
        if not keys:
            return ()
        with jax.named_scope(name):
            value = how(bundle(sources, gate))
        into.update({key: (value, number) for number, key in enumerate(keys)})
        return (value,)

    def part(layer, hops, begun=None, finish=True):
        return Part(layer, [(h, whose is mine, *whose[layer, h]) for whose in (mine, theirs) for h in hops], () if begun is None else (begun,), finish)

    def complete(layer):
        return [*range(chips - 1), -1] if layer in (0, -1) else [*range(chips)]

    state = {"outs": None}
    sums, used = {}, {d: [] for d in distances}

    def products(keys):
        parts = []
        for d in distances:
            hops = [h for h in complete(d) if (d, h) in keys and h not in used[d]]
            if hops:
                used[d] += hops
                parts.append(part(d, hops, sums.pop(d, None), len(used[d]) == len(complete(d))))
        parts.sort(key=lambda p: p.finish)
        state["outs"], kept = run(parts, outs=state["outs"])
        unfinished = [p for p in parts if not p.finish]
        sums.update({p.stage: s for p, s in zip(unfinished, kept, strict=True)})
        return kept[0] if unfinished else state["outs"][0]

    def tiny(value, number):
        at = 16 * (number % (ritz.shape[1] // 16))
        with jax.named_scope("token"):
            return moves.other(after(lax.slice(ritz, (0, at, 0), (1, at + 16, 128)), value))

    along_gate = gate = ()
    fresh = [(0, 0)]
    for r in range(1, final + 1):
        if r < cols - 1:
            layer, hop, step = r, 0, 1
        else:
            layer, hop, step = -1, r - (cols - 1), -1
        source = (layer - step, hop)
        z = move(lambda v: moves.along(v, step), mine, [source], [(layer, hop)], along_gate, f"along{layer}_{hop}")
        ring = [(d, r - d) for d in range(cols - 1) if 1 <= r - d <= (chips - 2 if d == 0 else chips - 1)]
        p = move(lambda v: moves.ring(v, 1), mine, [(d, h - 1) for d, h in ring], ring, gate, f"ring{r}")
        back = {1: [(0, -1)], final: [(-1, -1)]}.get(r, [])
        m = move(lambda v: moves.ring(v, -1), mine, [(d, 0) for d, _ in back], back, gate, f"back{r}")
        e = move(moves.other, theirs, fresh, fresh, gate, f"core{r}")
        fresh_before, fresh = fresh, [*ring, (layer, hop), *back]
        token = ()
        held = set(theirs) - set(fresh_before)
        if r >= chips:
            ran = products(held)
            if r == final:
                ran = products(set(theirs))
            token = (tiny(ran, r),)
        along_gate = (*p, *m, *e, *token, *(lefts if r == 1 else ()))
        gate = (*along_gate, *z)
    for key in [key for key in fresh if key != (layer, hop)]:
        move(moves.other, theirs, [key], [key], token, f"core_last{key[0]}_{key[1]}")
    products(set(theirs))
    move(moves.other, theirs, [(layer, hop)], [(layer, hop)], (), "core_end")
    products(set(theirs))
    return state["outs"]


def shards(rows, cols, orbitals, applied, ritz):
    moves = Moves(rows, cols)
    lefts = [x.reshape(x.shape[0], -1) for x in (orbitals, applied)]
    run = functools.partial(run_parts, rows=rows, cols=cols, lefts=lefts, like=orbitals)
    return (few_rounds if (moves.chips, cols) == (4, 4) else any_rounds)(moves, run, lefts, ritz)


def solution(mesh):
    rows, cols = mesh.shape["row"], mesh.shape["col"]
    whole = P(AXES, None, None)
    return jax.shard_map(
        functools.partial(shards, rows, cols),
        mesh=mesh,
        in_specs=(whole, whole, P(None, "row", "col")),
        out_specs=(whole, whole),
        check_vma=False,
    )
```
